32 devices in a mesh: lon: 8 (over z, core), lat: 4 (over y, x).
Axes of the slice: x: 2, y: 2, z: 4, core: 2. Of those that a mesh axis runs over, the one named last changes fastest.
Arguments:
- sample_collection: float32 [17, 6, 32, 1024], P(None, None, 'lat', 'lon'), may hold values from -5.5 to 5.5
- obs_index: int32 [4, 8, 128], P('lat', 'lon'), may hold values from 0 to 1023, as said below
- obs_count: int32 [4, 8], P('lat', 'lon'), may hold values from 42 to 128
- obs_value: float32 [4, 8, 128], P('lat', 'lon'), may hold values from -5 to 5
- obs_weight: float32 [4, 8, 128], P('lat', 'lon'), may hold values from 8 to 128
Outputs:
- analysis: float32 [17, 6, 32, 1024], P(None, None, 'lat', 'lon')
- analysis_spread: float32 [17, 17], replicated
The draws below stay inside these ranges and needn't reach their ends.
Inputs may be any that keep to these rules, and one draw needn't show every extreme that they name: `obs_index`: cell number within the tile, row-major over its 8 x 128 cells; slots at or past the tile's count are ignored.
All inputs are finite; a program needn't handle non-finite values.
Results may differ from the reference program's by a relative error of at most 0.00021.
Values sent between devices are 32-bit elements; how exact they have to be, the bound alone decides.
A program may use at most 64 MiB of HBM per device.

```python
import math
import jax
import jax.numpy as jnp
from jax import lax

UNCERTAINTY_DIRS = 16
MEMBERS = 17
FIELDS = 6
CX = 128
CY = 8
SUBSTEPS = 4
OBS_DEV = 128
NX = 1024
NY = 32
N_LON = 8
N_LAT = 4


def draw_sample_collection(key, part):
    key_base, key_common, key_rough = jax.random.split(key, 3)
    row_values = jnp.arange(NY, dtype=jnp.float32)
    scale = 0.3 * jnp.exp(math.log(3.0) * row_values / max(NY - 1, 1))
    scale = scale.reshape(1, 1, NY, 1)
    common = jax.random.truncated_normal(key_common, -3.0, 3.0, (MEMBERS, FIELDS, 1, 1), jnp.float32)
    base = 0.5 * jax.random.truncated_normal(key_base, -3.0, 3.0, (1, FIELDS, NY, NX), jnp.float32)
    rough = jax.random.truncated_normal(key_rough, -3.0, 3.0, (MEMBERS, FIELDS, NY, NX), jnp.float32)
    return base + scale * 0.7 * (common + rough)


def draw_obs_index(key, part):
    tiles = NY // CY * (NX // CX)
    key_cells, key_place = jax.random.split(jax.random.fold_in(key, 11))
    cells = jax.random.randint(key_cells, (tiles * OBS_DEV,), 0, CY * CX, jnp.int32)
    places = jax.random.permutation(key_place, tiles * OBS_DEV)
    cells = cells.at[places[0]].set(CY * CX - 1)
    cells = cells.at[places[1]].set(0)
    return cells.reshape(NY // CY, NX // CX, OBS_DEV)


def draw_obs_count(key, part):
    tiles = NY // CY * (NX // CX)
    least = OBS_DEV // 3
    key_level, key_each, key_place = jax.random.split(jax.random.fold_in(key, 23), 3)
    level = jax.random.randint(key_level, (), least, OBS_DEV + 1, jnp.int32)
    raw_bits = jax.random.randint(key_each, (tiles,), 0, 1 << 20, jnp.int32)
    counts = least + raw_bits % (level - least + 1)
    places = jax.random.permutation(key_place, tiles)
    counts = counts.at[places[0]].set(OBS_DEV)
    counts = counts.at[places[1]].set(least)
    return counts.reshape(NY // CY, NX // CX)


def draw_obs_value(key, part):
    tiles_lat = NY // CY
    tiles_lon = NX // CX
    key_shift, key_noise = jax.random.split(jax.random.fold_in(key, 37))
    shift = jax.random.uniform(key_shift, (), jnp.float32, -2.0, 2.0)
    noise = jax.random.truncated_normal(key_noise, -3.0, 3.0, (tiles_lat, tiles_lon, OBS_DEV), jnp.float32)
    return noise + shift


def steps_of(key, extent, shards, low, high):
    factor_of, own = 1.0, jax.random.fold_in(key, 6)
    for position, blocks in shards:
        steps = jnp.exp(jax.random.uniform(jax.random.fold_in(own, position), (blocks,), jnp.float32, low / len(shards), high / len(shards)))
        factor_of = factor_of * jnp.repeat(steps, extent[position] // blocks).reshape([-1 if axis == position else 1 for axis in range(len(extent))])
    return factor_of


def setup_inputs(seed: int = 0) -> dict:
    key_of = jax.random.split(jax.random.key(seed), 6)
    return {
        "sample_collection": draw_sample_collection(jax.random.fold_in(key_of[5], 71), 0),
        "obs_index": draw_obs_index(jax.random.fold_in(key_of[5], 71), 0),
        "obs_count": draw_obs_count(jax.random.fold_in(key_of[5], 71), 0),
        "obs_value": draw_obs_value(jax.random.fold_in(key_of[5], 71), 0),
        "obs_weight": jnp.clip(jnp.exp(math.log(128.0) - 2.7725887 * jax.random.uniform(key_of[4], (N_LAT, N_LON, OBS_DEV), jnp.float32) ** steps_of(key_of[4], (N_LAT, N_LON, OBS_DEV), ((0, 4), (1, 8)), -0.2, 0.2)), 8.0, 128.0),
    }


time_step = 0.15
coriolis_scale = 0.5
grav_low = 0.5
depth_top = 4.0
depth_low = 6.0
forget = 0.9
highest = lax.Precision.HIGHEST

def from_east(quantity):
    return quantity[..., 1:-1, 2:]

def from_west(quantity):
    return quantity[..., 1:-1, :-2]

def from_north(quantity):
    return quantity[..., 2:, 1:-1]

def from_south(quantity):
    return quantity[..., :-2, 1:-1]

def neighbour_mean(quantity):
    return 0.25 * (from_east(quantity) + from_west(quantity) + from_north(quantity) + from_south(quantity))

def zonal_slope(quantity):
    return 0.5 * (from_east(quantity) - from_west(quantity))

def merid_slope(quantity):
    return 0.5 * (from_north(quantity) - from_south(quantity))

def layer_update(thick, zonal, merid, pressure, rest_depth, coriolis):
    column = rest_depth + thick
    thick_new = neighbour_mean(thick) - time_step * (zonal_slope(column * zonal) + merid_slope(column * merid))
    zonal_here = zonal[..., 1:-1, 1:-1]
    merid_here = merid[..., 1:-1, 1:-1]
    zonal_new = neighbour_mean(zonal) - time_step * (zonal_here * zonal_slope(zonal) + merid_here * merid_slope(zonal) - coriolis * merid_here + zonal_slope(pressure))
    merid_new = neighbour_mean(merid) - time_step * (zonal_here * zonal_slope(merid) + merid_here * merid_slope(merid) + coriolis * zonal_here + merid_slope(pressure))
    return (thick_new, zonal_new, merid_new)

def advance(padded, coriolis):
    thick_top = padded[..., 0, :, :]
    thick_low = padded[..., 3, :, :]
    press_top = thick_top + thick_low
    press_low = press_top + grav_low * thick_low
    upper_layer = layer_update(thick_top, padded[..., 1, :, :], padded[..., 2, :, :], press_top, depth_top, coriolis)
    lower_layer = layer_update(thick_low, padded[..., 4, :, :], padded[..., 5, :, :], press_low, depth_low, coriolis)
    return jnp.stack(upper_layer + lower_layer, axis=-3)

def coriolis_rows(first_row, row_count, total_rows):
    row_values = first_row + jnp.arange(row_count, dtype=jnp.float32)
    return (coriolis_scale * (2.0 * (row_values + 0.5) / total_rows - 1.0)).reshape(row_count, 1)

def mode_space(obs_gram, obs_proj):
    identity = jnp.eye(UNCERTAINTY_DIRS, dtype=jnp.float32)
    gamma_matrix = identity - 1.0 / MEMBERS
    precision = UNCERTAINTY_DIRS / forget * gamma_matrix + obs_gram
    factor = jnp.linalg.cholesky(precision)
    weights = jax.scipy.linalg.cho_solve((factor, True), obs_proj)
    projector = jnp.concatenate([identity, jnp.zeros((1, UNCERTAINTY_DIRS), jnp.float32)], axis=0) - 1.0 / MEMBERS
    root_fix = identity + (math.sqrt(MEMBERS) - 1.0) / UNCERTAINTY_DIRS
    omega_matrix = jnp.dot(projector, root_fix, precision=highest)
    rotation = math.sqrt(UNCERTAINTY_DIRS) * jax.scipy.linalg.solve_triangular(factor.T, omega_matrix.T, lower=False)
    return (weights, rotation)

def reference(sample_collection, obs_index, obs_count, obs_value, obs_weight):
    coriolis = coriolis_rows(0.0, NY, NY)

    def sample_prediction(single_sample):
        for substep in range(SUBSTEPS):
            wrapped = jnp.concatenate([single_sample[..., -1:], single_sample, single_sample[..., :1]], axis=-1)
            padded = jnp.pad(wrapped, ((0, 0), (1, 1), (0, 0)))
            single_sample = advance(padded, coriolis)
        return single_sample
    prediction_integration = lax.map(sample_prediction, sample_collection)
    sample_average_vector = lax.optimization_barrier(jnp.mean(prediction_integration, axis=0))
    uncertainty_directions = prediction_integration[:UNCERTAINTY_DIRS] - sample_average_vector
    mode_gram = jnp.zeros((UNCERTAINTY_DIRS, UNCERTAINTY_DIRS), jnp.float32)
    for quantity in range(FIELDS):
        flat = uncertainty_directions[:, quantity].reshape(UNCERTAINTY_DIRS, -1)
        mode_gram = mode_gram + jnp.dot(flat, flat.T, precision=highest)
    interface_elevation = prediction_integration[:, 0] + prediction_integration[:, 3]
    tile_lat = jnp.arange(N_LAT, dtype=jnp.int32).reshape(N_LAT, 1, 1)
    tile_lon = jnp.arange(N_LON, dtype=jnp.int32).reshape(1, N_LON, 1)
    obs_rows = tile_lat * CY + obs_index // CX
    obs_columns = tile_lon * CX + obs_index % CX
    observed = interface_elevation[:, obs_rows, obs_columns].reshape(MEMBERS, -1)
    live_slots = (jnp.arange(OBS_DEV, dtype=jnp.int32).reshape(1, 1, OBS_DEV) < obs_count[:, :, None]).astype(jnp.float32)
    weight = (obs_weight * live_slots / (OBS_DEV * N_LAT * N_LON)).reshape(-1)
    obs_mean = lax.optimization_barrier(jnp.mean(observed, axis=0))
    anomaly = observed[:UNCERTAINTY_DIRS] - obs_mean
    innovation = obs_value.reshape(-1) - obs_mean
    weighted = anomaly * weight
    obs_gram = jnp.dot(weighted, anomaly.T, precision=highest)
    obs_proj = jnp.dot(weighted, innovation, precision=highest)
    weights, rotation = mode_space(obs_gram, obs_proj)
    coefficient = weights[:, None] + rotation
    pieces = []
    for quantity in range(FIELDS):
        flat = uncertainty_directions[:, quantity].reshape(UNCERTAINTY_DIRS, -1)
        update = jnp.dot(coefficient.T, flat, precision=highest).reshape(MEMBERS, NY, NX)
        pieces.append(sample_average_vector[quantity] + update)
    analysis = jnp.stack(pieces, axis=1)
    spread = jnp.dot(rotation.T, jnp.dot(mode_gram, rotation, precision=highest), precision=highest) / (FIELDS * NY * NX)
    return (analysis, spread)
```

```python
import functools
import math

import jax
import jax.numpy as jnp
import numpy as np
from jax import lax
from jax.experimental import pallas as pl
from jax.experimental.pallas import tpu as pltpu
from jax.sharding import PartitionSpec as P

SUBSTEPS = 4

time_step = 0.15
coriolis_scale = 0.5
grav_low = 0.5
depth_top = 4.0
depth_low = 6.0
forget = 0.9
highest = lax.Precision.HIGHEST
MESH = pl.DeviceIdType.MESH

SYS = 32


def split2(x):
    high = x.astype(jnp.bfloat16)
    low = (x - high.astype(jnp.float32)).astype(jnp.bfloat16)
    return high, low


def split3(x):
    high = x.astype(jnp.bfloat16)
    rest = x - high.astype(jnp.float32)
    mid = rest.astype(jnp.bfloat16)
    low = (rest - mid.astype(jnp.float32)).astype(jnp.bfloat16)
    return high, mid, low


def dot(a, b):
    return jnp.dot(a, b, preferred_element_type=jnp.float32)


def dot_nt(a, b, precision=None):
    return lax.dot_general(
        a, b, (((1,), (1,)), ((), ())), precision=precision, preferred_element_type=jnp.float32
    )


def kernel(
    dims, x_ref, index_ref, count_ref, value_ref, weight_ref, system_ref, omega_ref,
    out_ref, spread_ref,
    state, send_low, send_high, send_cols, from_north, from_south, from_east, from_west,
    surface, selector, means, modes, parts, gather_lon, gather_lat,
    halo_send, halo_recv, lon_send, lon_recv, lat_send, lat_recv,
):
    members, fields, rows, cols, n_lat, n_lon = dims
    dirs = members - 1
    tiles = members * fields
    cells = rows * cols
    slots = index_ref.shape[1]
    me_lon, me_lat = lax.axis_index("lon"), lax.axis_index("lat")

    def lon_at(d):
        return (lax.rem(me_lon + d + n_lon, n_lon), me_lat)

    def lat_at(d):
        return (me_lon, lax.rem(me_lat + d + n_lat, n_lat))

    partners = [lon_at(d) for d in range(1, n_lon)] + [lat_at(d) for d in range(1, n_lat)]
    barrier = pltpu.get_barrier_semaphore()
    for partner in partners:
        pl.semaphore_signal(barrier, inc=1, device_id=partner, device_id_type=MESH)

    lane = lax.broadcasted_iota(jnp.int32, (rows, cols), 1)
    row = lax.broadcasted_iota(jnp.int32, (rows, cols), 0)
    half = lane // 2
    first_lane, last_lane = lane == 0, lane == cols - 1
    first_row, last_row = row == 0, row == rows - 1
    even_lane = (lane - 2 * half) == 0
    row_number = (row + me_lat * rows).astype(jnp.float32)
    coriolis = coriolis_scale * (2.0 * (row_number + 0.5) / (rows * n_lat) - 1.0)
    turn = time_step * coriolis
    ghost = 0.5 * time_step

    def pack(packed, tile, quantity):
        base = tile - tile % 2
        moved = pltpu.roll(quantity, base + 1, 1)
        packed[tile % 2] = jnp.where(half == base // 2, moved, packed[tile % 2])

    def put_edges(slot, tile, quantity):
        send_low[slot, tile : tile + 1, :] = quantity[0:1, :]
        send_high[slot, tile : tile + 1, :] = quantity[rows - 1 : rows, :]

    def put_cols(slot, packed):
        send_cols[slot, 0:rows, :] = packed[0]
        send_cols[slot, rows : 2 * rows, :] = packed[1]

    packed = [jnp.zeros((rows, cols), jnp.float32)] * 2
    for tile in range(tiles):
        quantity = x_ref[tile * rows : (tile + 1) * rows, :]
        state[0, tile * rows : (tile + 1) * rows, :] = quantity
        put_edges(0, tile, quantity)
        pack(packed, tile, quantity)
    put_cols(0, packed)

    for r in range(rows):
        cell = lax.broadcasted_iota(jnp.int32, (cols, slots), 0) + r * cols
        hit = jnp.where(cell == index_ref[...], 1.0, 0.0)
        selector[r * cols : (r + 1) * cols, :] = hit.astype(jnp.bfloat16)
    live = lax.broadcasted_iota(jnp.int32, (1, slots), 1) < count_ref[...]
    weight = jnp.where(live, weight_ref[...], 0.0) / (slots * n_lat * n_lon)
    surface[...] = jnp.zeros_like(surface)

    pl.semaphore_wait(barrier, len(partners))

    def substep(step, carry):
        now, later = lax.rem(step, 2), lax.rem(step + 1, 2)
        copies = []
        for number, (source, target, device) in enumerate((
            (send_low, from_north, lat_at(-1)),
            (send_high, from_south, lat_at(1)),
            (send_cols, from_east, lon_at(-1)),
            (send_cols, from_west, lon_at(1)),
        )):
            copy = pltpu.make_async_remote_copy(
                src_ref=source.at[step],
                dst_ref=target.at[step],
                send_sem=halo_send.at[step, number],
                recv_sem=halo_recv.at[step, number],
                device_id=device,
                device_id_type=MESH,
            )
            copy.start()
            copies.append(copy)
        for copy in copies:
            copy.wait()
        north_on = jnp.where(me_lat < n_lat - 1, 1.0, 0.0)
        south_on = jnp.where(me_lat > 0, 1.0, 0.0)
        columns = []
        for parity in range(2):
            east = pltpu.roll(from_east[step, parity * rows : (parity + 1) * rows, :], cols - 1, 1)
            west = pltpu.roll(from_west[step, parity * rows : (parity + 1) * rows, :], 1, 1)
            columns.append(jnp.where(even_lane, east, west))

        packed = [jnp.zeros((rows, cols), jnp.float32)] * 2
        for member in range(members):
            here, east, west, north, south = [], [], [], [], []
            for field in range(fields):
                tile = member * fields + field
                base = tile - tile % 2
                q = state[now, tile * rows : (tile + 1) * rows, :]
                side = pltpu.roll(columns[tile % 2], cols - 1 - base, 1)
                above = from_north[step, tile : tile + 1, :] * north_on
                below = from_south[step, tile : tile + 1, :] * south_on
                here.append(q)
                east.append(jnp.where(last_lane, side, pltpu.roll(q, cols - 1, 1)))
                west.append(jnp.where(first_lane, side, pltpu.roll(q, 1, 1)))
                north.append(jnp.where(last_row, above, pltpu.roll(q, rows - 1, 0)))
                south.append(jnp.where(first_row, below, pltpu.roll(q, 1, 0)))
            dx = [e - w for e, w in zip(east, west)]
            dy = [n - s for n, s in zip(north, south)]
            mean = [0.25 * ((e + w) + (n + s)) for e, w, n, s in zip(east, west, north, south)]
            px_top, py_top = dx[0] + dx[3], dy[0] + dy[3]
            px = (px_top, px_top + grav_low * dx[3])
            py = (py_top, py_top + grav_low * dy[3])
            after = []
            for layer, depth in enumerate((depth_top, depth_low)):
                h, u, v = 3 * layer, 3 * layer + 1, 3 * layer + 2
                flux = ((depth + east[h]) * east[u] - (depth + west[h]) * west[u]) + (
                    (depth + north[h]) * north[v] - (depth + south[h]) * south[v]
                )
                after.append(mean[h] - ghost * flux)
                after.append(
                    mean[u]
                    - ghost * (here[u] * dx[u] + here[v] * dy[u] + px[layer])
                    + turn * here[v]
                )
                after.append(
                    mean[v]
                    - ghost * (here[u] * dx[v] + here[v] * dy[v] + py[layer])
                    - turn * here[u]
                )
            for field in range(fields):
                tile = member * fields + field
                state[later, tile * rows : (tile + 1) * rows, :] = after[field]
                put_edges(step + 1, tile, after[field])
                pack(packed, tile, after[field])
            surface[member * rows : (member + 1) * rows, :] = after[0] + after[3]
        put_cols(step + 1, packed)
        return carry

    lax.fori_loop(0, SUBSTEPS, substep, 0)
    final = SUBSTEPS % 2

    pad = surface.shape[0] // rows
    observed = jnp.zeros((3 * pad, slots), jnp.float32)
    for r in range(rows):
        level = surface[pl.ds(r, pad, stride=rows), :]
        observed += dot(
            jnp.concatenate(split3(level), axis=0), selector[r * cols : (r + 1) * cols, :]
        )
    observed = observed[0:pad] + observed[pad : 2 * pad] + observed[2 * pad : 3 * pad]
    obs_mean = jnp.sum(observed, axis=0, keepdims=True) * (1.0 / members)
    anomaly = observed[0:dirs] - obs_mean
    innovation = value_ref[...] - obs_mean
    top = lax.broadcasted_iota(jnp.int32, (8, slots), 0) == 0
    right = jnp.concatenate(
        [jnp.zeros((SYS, slots), jnp.float32), anomaly, jnp.where(top, innovation, 0.0)], axis=0
    )
    gather_lon[me_lon] = jnp.zeros(gather_lon.shape[1:], jnp.float32)
    gather_lon[me_lon, 0:dirs, 0 : right.shape[0]] = dot_nt(anomaly * weight, right, highest)

    for field in range(fields):
        total = state[final, field * rows : (field + 1) * rows, :]
        for member in range(1, members):
            at = (member * fields + field) * rows
            total = total + state[final, at : at + rows, :]
        total = total * (1.0 / members)
        means[field * rows : (field + 1) * rows, :] = total
        for member in range(dirs):
            at = (member * fields + field) * rows
            modes[at : at + rows, :] = state[final, at : at + rows, :] - total
    for line in range(fields * rows):
        high, low = split2(modes[pl.ds(line, dirs, stride=fields * rows), :])
        parts[0:dirs, line * cols : (line + 1) * cols] = high
        parts[dirs : 2 * dirs, line * cols : (line + 1) * cols] = low
    high, low = parts[0:dirs, :], parts[dirs : 2 * dirs, :]
    gather_lon[me_lon, dirs : 2 * dirs, 0:dirs] = (
        dot_nt(high, high) + dot_nt(high, low) + dot_nt(low, high)
    )

    def gather(buffer, me, count, device_of, send, recv):
        copies = []
        for d in range(1, count):
            copy = pltpu.make_async_remote_copy(
                src_ref=buffer.at[me],
                dst_ref=buffer.at[me],
                send_sem=send.at[d],
                recv_sem=recv.at[me],
                device_id=device_of(d),
                device_id_type=MESH,
            )
            copy.start()
            copies.append(copy)
        for d in range(1, count):
            other = lax.rem(me + d, count)
            pltpu.make_async_remote_copy(
                src_ref=buffer.at[other],
                dst_ref=buffer.at[other],
                send_sem=send.at[d],
                recv_sem=recv.at[other],
                device_id=device_of(d),
                device_id_type=MESH,
            ).wait_recv()
        for copy in copies:
            copy.wait_send()
        total = buffer[0]
        for i in range(1, count):
            total = total + buffer[i]
        return total

    gather_lat[me_lat] = gather(gather_lon, me_lon, n_lon, lon_at, lon_send, lon_recv)
    total = gather(gather_lat, me_lat, n_lat, lat_at, lat_send, lat_recv)

    system = total[0:dirs] + system_ref[...]
    mode_gram = total[dirs : 2 * dirs, 0:dirs]
    below = lax.broadcasted_iota(jnp.int32, system.shape, 0)
    across = lax.broadcasted_iota(jnp.int32, system.shape, 1)
    for j in range(dirs):
        pivot = system[j : j + 1, SYS + j : SYS + j + 1]
        column = system[:, SYS + j : SYS + j + 1]
        factor = jnp.where(below > j, column / pivot, 0.0)
        system = system - factor * system[j : j + 1, :]
    diagonal = jnp.sum(jnp.where(across == below + SYS, system, 0.0), axis=1, keepdims=True)
    system = system / jnp.sqrt(diagonal)
    solved = system[:, SYS + dirs : SYS + dirs + 1]
    inverse = system[:, 0:dirs]
    weights = jnp.sum(solved * inverse, axis=0, keepdims=True)
    rotation = jnp.dot(
        omega_ref[...], inverse, precision=highest, preferred_element_type=jnp.float32
    )
    spread = dot_nt(
        jnp.dot(rotation, mode_gram, precision=highest, preferred_element_type=jnp.float32),
        rotation,
        highest,
    )
    spread_ref[...] = spread * (1.0 / (fields * cells * n_lat * n_lon))

    c_high, c_low = split2(rotation + weights)
    for field in range(fields):
        block = pl.ds(field * cells, cells)
        high = parts[0:dirs, block]
        update = dot(c_high, high) + dot(c_high, parts[dirs : 2 * dirs, block]) + dot(c_low, high)
        for r in range(rows):
            line = field * rows + r
            out_ref[pl.ds(line, members, stride=fields * rows), :] = (
                update[:, r * cols : (r + 1) * cols] + means[line : line + 1, :]
            )


def constants(members):
    dirs = members - 1
    identity = np.eye(dirs)
    system = np.zeros((dirs, 128))
    system[:, 0:dirs] = identity
    system[:, SYS : SYS + dirs] = dirs / forget * (identity - 1.0 / members)
    projector = np.concatenate([identity, np.zeros((1, dirs))], axis=0) - 1.0 / members
    omega = projector @ (identity + (math.sqrt(members) - 1.0) / dirs)
    return system.astype(np.float32), (math.sqrt(dirs) * omega).astype(np.float32)


def on_device(n_lat, n_lon, sample_collection, obs_index, obs_count, obs_value, obs_weight):
    members, fields, rows, cols = sample_collection.shape
    slots = obs_index.shape[-1]
    dirs, tiles = members - 1, members * fields
    padded_tiles = -(-tiles // 8) * 8
    pad = -(-members // 16) * 16
    system, omega = constants(members)
    f32 = jnp.float32
    dims = (members, fields, rows, cols, n_lat, n_lon)
    analysis, spread = pl.pallas_call(
        functools.partial(kernel, dims),
        out_shape=(
            jax.ShapeDtypeStruct((tiles * rows, cols), f32),
            jax.ShapeDtypeStruct((members, members), f32),
        ),
        in_specs=[pl.BlockSpec(memory_space=pltpu.VMEM)] * 7,
        out_specs=(pl.BlockSpec(memory_space=pltpu.VMEM),) * 2,
        scratch_shapes=[
            pltpu.VMEM((2, tiles * rows, cols), f32),
            pltpu.VMEM((SUBSTEPS + 1, padded_tiles, cols), f32),
            pltpu.VMEM((SUBSTEPS + 1, padded_tiles, cols), f32),
            pltpu.VMEM((SUBSTEPS + 1, 2 * rows, cols), f32),
            pltpu.VMEM((SUBSTEPS, padded_tiles, cols), f32),
            pltpu.VMEM((SUBSTEPS, padded_tiles, cols), f32),
            pltpu.VMEM((SUBSTEPS, 2 * rows, cols), f32),
            pltpu.VMEM((SUBSTEPS, 2 * rows, cols), f32),
            pltpu.VMEM((pad * rows, cols), f32),
            pltpu.VMEM((rows * cols, slots), jnp.bfloat16),
            pltpu.VMEM((fields * rows, cols), f32),
            pltpu.VMEM((dirs * fields * rows, cols), f32),
            pltpu.VMEM((2 * dirs, fields * rows * cols), jnp.bfloat16),
            pltpu.VMEM((n_lon, 2 * dirs, 128), f32),
            pltpu.VMEM((n_lat, 2 * dirs, 128), f32),
            pltpu.SemaphoreType.DMA((SUBSTEPS, 4)),
            pltpu.SemaphoreType.DMA((SUBSTEPS, 4)),
            pltpu.SemaphoreType.DMA((n_lon,)),
            pltpu.SemaphoreType.DMA((n_lon,)),
            pltpu.SemaphoreType.DMA((n_lat,)),
            pltpu.SemaphoreType.DMA((n_lat,)),
        ],
        compiler_params=pltpu.CompilerParams(
            collective_id=0, has_side_effects=True, vmem_limit_bytes=32 * 1024 * 1024
        ),
    )(
        sample_collection.reshape(tiles * rows, cols),
        obs_index.reshape(1, slots),
        obs_count.reshape(1, 1),
        obs_value.reshape(1, slots),
        obs_weight.reshape(1, slots),
        jnp.asarray(system),
        jnp.asarray(omega),
    )
    return analysis.reshape(sample_collection.shape), spread


def solution(mesh):
    return jax.shard_map(
        functools.partial(on_device, mesh.shape["lat"], mesh.shape["lon"]),
        mesh=mesh,
        in_specs=(
            P(None, None, "lat", "lon"),
            P("lat", "lon", None),
            P("lat", "lon"),
            P("lat", "lon", None),
            P("lat", "lon", None),
        ),
        out_specs=(P(None, None, "lat", "lon"), P()),
        check_vma=False,
    )
```

```python
import functools
import math

import jax
import jax.numpy as jnp
from jax import lax
from jax.experimental import pallas as pl
from jax.experimental.pallas import tpu as pltpu
from jax.sharding import PartitionSpec as P

SUBSTEPS = 4

time_step = 0.15
coriolis_scale = 0.5
grav_low = 0.5
depth_top = 4.0
depth_low = 6.0
forget = 0.9
highest = lax.Precision.HIGHEST
MESH = pl.DeviceIdType.MESH

SYS = 32
BATCH = 4


def split2(x):
    high = x.astype(jnp.bfloat16)
    low = (x - high.astype(jnp.float32)).astype(jnp.bfloat16)
    return high, low


def split3(x):
    high = x.astype(jnp.bfloat16)
    rest = x - high.astype(jnp.float32)
    mid = rest.astype(jnp.bfloat16)
    low = (rest - mid.astype(jnp.float32)).astype(jnp.bfloat16)
    return high, mid, low


def dot(a, b):
    return jnp.dot(a, b, preferred_element_type=jnp.float32)


def dot_nt(a, b, precision=None):
    return lax.dot_general(
        a, b, (((1,), (1,)), ((), ())), precision=precision, preferred_element_type=jnp.float32
    )


def kernel(
    dims, x_hbm, index_hbm, count_hbm, value_hbm, weight_hbm,
    out_ref, spread_ref,
    index_ref, count_ref, value_ref, weight_ref, state, send_low, send_high, send_cols, from_north, from_south, from_east, from_west,
    surface, selector, means, modes, parts,
    obs_lon, obs_lat, gram_lon, gram_lat, load_sem, halo_send, halo_recv,
    obs_lon_send, obs_lon_recv, obs_lat_send, obs_lat_recv,
    gram_lon_send, gram_lon_recv, gram_lat_send, gram_lat_recv,
):
    members, fields, rows, cols, n_lat, n_lon = dims
    dirs = members - 1
    tiles = members * fields
    cells = rows * cols
    slots = index_ref.shape[1]
    me_lon, me_lat = lax.axis_index("lon"), lax.axis_index("lat")

    def lon_at(d):
        return (lax.rem(me_lon + d + n_lon, n_lon), me_lat)

    def lat_at(d):
        return (me_lon, lax.rem(me_lat + d + n_lat, n_lat))

    partners = [lon_at(d) for d in range(1, n_lon)] + [lat_at(d) for d in range(1, n_lat)]
    barrier = pltpu.get_barrier_semaphore()
    for partner in partners:
        pl.semaphore_signal(barrier, inc=1, device_id=partner, device_id_type=MESH)

    loads = [
        pltpu.make_async_copy(source, target, load_sem.at[number])
        for number, (source, target) in enumerate((
            (x_hbm, state.at[0]),
            (index_hbm, index_ref),
            (count_hbm, count_ref),
            (value_hbm, value_ref),
            (weight_hbm, weight_ref),
        ))
    ]
    for load in loads:
        load.start()

    @pl.when(me_lat == n_lat - 1)
    def _():
        from_north[...] = jnp.zeros_like(from_north)

    @pl.when(me_lat == 0)
    def _():
        from_south[...] = jnp.zeros_like(from_south)

    surface[...] = jnp.zeros_like(surface)
    lane = lax.broadcasted_iota(jnp.int32, (rows, cols), 1)
    row = lax.broadcasted_iota(jnp.int32, (rows, cols), 0)
    half = lane // 2
    first_lane, last_lane = lane == 0, lane == cols - 1
    first_row, last_row = row == 0, row == rows - 1
    even_lane = (lane - 2 * half) == 0
    row_number = (row + me_lat * rows).astype(jnp.float32)
    coriolis = coriolis_scale * (2.0 * (row_number + 0.5) / (rows * n_lat) - 1.0)
    turn = time_step * coriolis
    ghost = 0.5 * time_step

    def pack(packed, tile, quantity):
        base = tile - tile % 2
        moved = pltpu.roll(quantity, base + 1, 1)
        packed[tile % 2] = jnp.where(half == base // 2, moved, packed[tile % 2])

    def put_edges(slot, tile, quantity):
        send_low[slot, tile : tile + 1, :] = quantity[0:1, :]
        send_high[slot, tile : tile + 1, :] = quantity[rows - 1 : rows, :]

    def put_cols(slot, packed):
        send_cols[slot, 0:rows, :] = packed[0]
        send_cols[slot, rows : 2 * rows, :] = packed[1]

    for load in loads:
        load.wait()
    packed = [jnp.zeros((rows, cols), jnp.float32)] * 2
    for tile in range(tiles):
        quantity = state[0, tile * rows : (tile + 1) * rows, :]
        put_edges(0, tile, quantity)
        pack(packed, tile, quantity)
    put_cols(0, packed)

    pl.semaphore_wait(barrier, len(partners))

    def exchange(step):
        copies = []
        for number, (source, target, device) in enumerate((
            (send_low, from_north, lat_at(-1)),
            (send_high, from_south, lat_at(1)),
            (send_cols, from_east, lon_at(-1)),
            (send_cols, from_west, lon_at(1)),
        )):
            copies.append(pltpu.make_async_remote_copy(
                src_ref=source.at[step],
                dst_ref=target.at[step],
                send_sem=halo_send.at[step, number],
                recv_sem=halo_recv.at[step, number],
                device_id=device,
                device_id_type=MESH,
            ))
        return copies

    def exchange_start(step):
        to_south, to_north, to_west, to_east = exchange(step)

        @pl.when(me_lat > 0)
        def _():
            to_south.start()

        @pl.when(me_lat < n_lat - 1)
        def _():
            to_north.start()

        to_west.start()
        to_east.start()

    def exchange_end(step):
        to_south, to_north, to_west, to_east = exchange(step)

        @pl.when(me_lat > 0)
        def _():
            to_south.wait_send()
            to_north.wait_recv()

        @pl.when(me_lat < n_lat - 1)
        def _():
            to_north.wait_send()
            to_south.wait_recv()

        to_west.wait()
        to_east.wait()

    exchange_start(0)
    for r in range(rows):
        cell = lax.broadcasted_iota(jnp.int32, (cols, slots), 0) + r * cols
        hit = jnp.where(cell == index_ref[...], 1.0, 0.0)
        selector[r * cols : (r + 1) * cols, :] = hit.astype(jnp.bfloat16)
    live = lax.broadcasted_iota(jnp.int32, (1, slots), 1) < count_ref[...]
    weight = jnp.where(live, weight_ref[...], 0.0) / (slots * n_lat * n_lon)

    def substep(step, carry):
        now, later = lax.rem(step, 2), lax.rem(step + 1, 2)
        exchange_end(step)
        columns = []
        for parity in range(2):
            east = pltpu.roll(from_east[step, parity * rows : (parity + 1) * rows, :], cols - 1, 1)
            west = pltpu.roll(from_west[step, parity * rows : (parity + 1) * rows, :], 1, 1)
            columns.append(jnp.where(even_lane, east, west))

        packed = [jnp.zeros((rows, cols), jnp.float32)] * 2
        for member in range(members):
            here, east, west, north, south = [], [], [], [], []
            for field in range(fields):
                tile = member * fields + field
                base = tile - tile % 2
                q = state[now, tile * rows : (tile + 1) * rows, :]
                side = pltpu.roll(columns[tile % 2], cols - 1 - base, 1)
                above = from_north[step, tile : tile + 1, :]
                below = from_south[step, tile : tile + 1, :]
                here.append(q)
                east.append(jnp.where(last_lane, side, pltpu.roll(q, cols - 1, 1)))
                west.append(jnp.where(first_lane, side, pltpu.roll(q, 1, 1)))
                north.append(jnp.where(last_row, above, pltpu.roll(q, rows - 1, 0)))
                south.append(jnp.where(first_row, below, pltpu.roll(q, 1, 0)))
            dx = [e - w for e, w in zip(east, west)]
            dy = [n - s for n, s in zip(north, south)]
            mean = [0.25 * ((e + w) + (n + s)) for e, w, n, s in zip(east, west, north, south)]
            px_top, py_top = dx[0] + dx[3], dy[0] + dy[3]
            px = (px_top, px_top + grav_low * dx[3])
            py = (py_top, py_top + grav_low * dy[3])
            after = []
            for layer, depth in enumerate((depth_top, depth_low)):
                h, u, v = 3 * layer, 3 * layer + 1, 3 * layer + 2
                flux = ((depth + east[h]) * east[u] - (depth + west[h]) * west[u]) + (
                    (depth + north[h]) * north[v] - (depth + south[h]) * south[v]
                )
                after.append(mean[h] - ghost * flux)
                after.append(
                    mean[u]
                    - ghost * (here[u] * dx[u] + here[v] * dy[u] + px[layer])
                    + turn * here[v]
                )
                after.append(
                    mean[v]
                    - ghost * (here[u] * dx[v] + here[v] * dy[v] + py[layer])
                    - turn * here[u]
                )
            for field in range(fields):
                tile = member * fields + field
                state[later, tile * rows : (tile + 1) * rows, :] = after[field]
                put_edges(step + 1, tile, after[field])
                pack(packed, tile, after[field])
            surface[member * rows : (member + 1) * rows, :] = after[0] + after[3]
        put_cols(step + 1, packed)

        @pl.when(step + 1 < SUBSTEPS)
        def _():
            exchange_start(step + 1)

        return carry

    lax.fori_loop(0, SUBSTEPS, substep, 0)
    final = SUBSTEPS % 2

    def gather(buffer, me, count, device_of, send, recv):
        copies = []
        for d in range(1, count):
            copy = pltpu.make_async_remote_copy(
                src_ref=buffer.at[me],
                dst_ref=buffer.at[me],
                send_sem=send.at[d],
                recv_sem=recv.at[me],
                device_id=device_of(d),
                device_id_type=MESH,
            )
            copy.start()
            copies.append(copy)

        def total():
            for d in range(1, count):
                other = lax.rem(me + d, count)
                pltpu.make_async_remote_copy(
                    src_ref=buffer.at[other],
                    dst_ref=buffer.at[other],
                    send_sem=send.at[d],
                    recv_sem=recv.at[other],
                    device_id=device_of(d),
                    device_id_type=MESH,
                ).wait_recv()
            for copy in copies:
                copy.wait_send()
            result = buffer[0]
            for i in range(1, count):
                result = result + buffer[i]
            return result

        return total

    pad = surface.shape[0] // rows
    observed = jnp.zeros((3 * pad, slots), jnp.float32)
    for r in range(rows):
        level = surface[pl.ds(r, pad, stride=rows), :]
        observed += dot(
            jnp.concatenate(split3(level), axis=0), selector[r * cols : (r + 1) * cols, :]
        )
    observed = observed[0:pad] + observed[pad : 2 * pad] + observed[2 * pad : 3 * pad]
    obs_mean = jnp.sum(observed, axis=0, keepdims=True) * (1.0 / members)
    anomaly = observed[0:dirs] - obs_mean
    innovation = value_ref[...] - obs_mean
    top = lax.broadcasted_iota(jnp.int32, (8, slots), 0) == 0
    right = jnp.concatenate(
        [jnp.zeros((SYS, slots), jnp.float32), anomaly, jnp.where(top, innovation, 0.0)], axis=0
    )
    obs_lon[me_lon] = jnp.zeros(obs_lon.shape[1:], jnp.float32)
    obs_lon[me_lon, :, 0 : right.shape[0]] = dot_nt(anomaly * weight, right, highest)
    obs_on_lon = gather(obs_lon, me_lon, n_lon, lon_at, obs_lon_send, obs_lon_recv)

    for field in range(fields):
        total = state[final, field * rows : (field + 1) * rows, :]
        for member in range(1, members):
            at = (member * fields + field) * rows
            total = total + state[final, at : at + rows, :]
        total = total * (1.0 / members)
        means[field * rows : (field + 1) * rows, :] = total
        for member in range(dirs):
            at = (member * fields + field) * rows
            modes[at : at + rows, :] = state[final, at : at + rows, :] - total
    for line in range(fields * rows):
        high, low = split2(modes[pl.ds(line, dirs, stride=fields * rows), :])
        parts[0:dirs, line * cols : (line + 1) * cols] = high
        parts[dirs : 2 * dirs, line * cols : (line + 1) * cols] = low
    high, low = parts[0:dirs, :], parts[dirs : 2 * dirs, :]
    gram_lon[me_lon] = jnp.zeros(gram_lon.shape[1:], jnp.float32)
    gram_lon[me_lon, :, 0:dirs] = dot_nt(high, high) + dot_nt(high, low) + dot_nt(low, high)
    gram_on_lon = gather(gram_lon, me_lon, n_lon, lon_at, gram_lon_send, gram_lon_recv)

    obs_lat[me_lat] = obs_on_lon()
    obs_on_lat = gather(obs_lat, me_lat, n_lat, lat_at, obs_lat_send, obs_lat_recv)
    gram_lat[me_lat] = gram_on_lon()
    gram_on_lat = gather(gram_lat, me_lat, n_lat, lat_at, gram_lat_send, gram_lat_recv)

    below = lax.broadcasted_iota(jnp.int32, (dirs, 128), 0)
    across = lax.broadcasted_iota(jnp.int32, (dirs, 128), 1)
    identity = jnp.where(across == below, 1.0, 0.0)
    inside = (across >= SYS) & (across < SYS + dirs)
    gamma = jnp.where(across == below + SYS, 1.0, 0.0) - jnp.where(inside, 1.0 / members, 0.0)
    system = obs_on_lat() + (identity + dirs / forget * gamma)
    for start in range(0, dirs, BATCH):
        batch = [
            jnp.broadcast_to(system[:, SYS + j : SYS + j + 1], system.shape)
            for j in range(start, start + BATCH)
        ]
        for i in range(BATCH):
            j = start + i
            factor = jnp.where(below > j, batch[i] * (1.0 / batch[i][j : j + 1, :]), 0.0)
            for k in range(i + 1, BATCH):
                batch[k] = batch[k] - factor * batch[k][j : j + 1, :]
            system = system - factor * system[j : j + 1, :]
    diagonal = jnp.sum(jnp.where(across == below + SYS, system, 0.0), axis=1, keepdims=True)
    system = system / jnp.sqrt(diagonal)
    solved = system[:, SYS + dirs : SYS + dirs + 1]
    inverse = system[:, 0:dirs]
    weights = jnp.sum(solved * inverse, axis=0, keepdims=True)
    shift = (math.sqrt(members) - 1.0) / dirs
    body = (shift - 1.0) / members
    tail = -math.sqrt(members) / members
    place = lax.broadcasted_iota(jnp.int32, (members, dirs), 0)
    mode = lax.broadcasted_iota(jnp.int32, (members, dirs), 1)
    omega = jnp.where(place == dirs, tail, jnp.where(place == mode, 1.0 + body, body))
    rotation = jnp.dot(
        math.sqrt(dirs) * omega, inverse, precision=highest, preferred_element_type=jnp.float32
    )
    c_high, c_low = split2(rotation + weights)
    for field in range(fields):
        block = pl.ds(field * cells, cells)
        high = parts[0:dirs, block]
        update = dot(c_high, high) + dot(c_high, parts[dirs : 2 * dirs, block]) + dot(c_low, high)
        for r in range(rows):
            line = field * rows + r
            out_ref[pl.ds(line, members, stride=fields * rows), :] = (
                update[:, r * cols : (r + 1) * cols] + means[line : line + 1, :]
            )

    mode_gram = gram_on_lat()[:, 0:dirs]
    spread = dot_nt(
        jnp.dot(rotation, mode_gram, precision=highest, preferred_element_type=jnp.float32),
        rotation,
        highest,
    )
    spread_ref[...] = spread * (1.0 / (fields * cells * n_lat * n_lon))


def on_device(n_lat, n_lon, sample_collection, obs_index, obs_count, obs_value, obs_weight):
    members, fields, rows, cols = sample_collection.shape
    slots = obs_index.shape[-1]
    dirs, tiles = members - 1, members * fields
    padded_tiles = -(-tiles // 8) * 8
    pad = -(-members // 16) * 16
    f32 = jnp.float32
    dims = (members, fields, rows, cols, n_lat, n_lon)
    analysis, spread = pl.pallas_call(
        functools.partial(kernel, dims),
        out_shape=(
            jax.ShapeDtypeStruct((tiles * rows, cols), f32),
            jax.ShapeDtypeStruct((members, members), f32),
        ),
        in_specs=[pl.BlockSpec(memory_space=pl.ANY)] * 5,
        out_specs=(pl.BlockSpec(memory_space=pltpu.VMEM),) * 2,
        scratch_shapes=[
            pltpu.VMEM((1, slots), jnp.int32),
            pltpu.VMEM((1, 1), jnp.int32),
            pltpu.VMEM((1, slots), f32),
            pltpu.VMEM((1, slots), f32),
            pltpu.VMEM((2, tiles * rows, cols), f32),
            pltpu.VMEM((SUBSTEPS + 1, padded_tiles, cols), f32),
            pltpu.VMEM((SUBSTEPS + 1, padded_tiles, cols), f32),
            pltpu.VMEM((SUBSTEPS + 1, 2 * rows, cols), f32),
            pltpu.VMEM((SUBSTEPS, padded_tiles, cols), f32),
            pltpu.VMEM((SUBSTEPS, padded_tiles, cols), f32),
            pltpu.VMEM((SUBSTEPS, 2 * rows, cols), f32),
            pltpu.VMEM((SUBSTEPS, 2 * rows, cols), f32),
            pltpu.VMEM((pad * rows, cols), f32),
            pltpu.VMEM((rows * cols, slots), jnp.bfloat16),
            pltpu.VMEM((fields * rows, cols), f32),
            pltpu.VMEM((dirs * fields * rows, cols), f32),
            pltpu.VMEM((2 * dirs, fields * rows * cols), jnp.bfloat16),
            pltpu.VMEM((n_lon, dirs, 128), f32),
            pltpu.VMEM((n_lat, dirs, 128), f32),
            pltpu.VMEM((n_lon, dirs, 128), f32),
            pltpu.VMEM((n_lat, dirs, 128), f32),
            pltpu.SemaphoreType.DMA((5,)),
            pltpu.SemaphoreType.DMA((SUBSTEPS, 4)),
            pltpu.SemaphoreType.DMA((SUBSTEPS, 4)),
        ]
        + [pltpu.SemaphoreType.DMA((n,)) for n in (n_lon, n_lon, n_lat, n_lat) * 2],
        compiler_params=pltpu.CompilerParams(
            collective_id=0, has_side_effects=True, vmem_limit_bytes=32 * 1024 * 1024
        ),
    )(
        sample_collection.reshape(tiles * rows, cols),
        obs_index.reshape(1, slots),
        obs_count.reshape(1, 1),
        obs_value.reshape(1, slots),
        obs_weight.reshape(1, slots),
    )
    return analysis.reshape(sample_collection.shape), spread


def solution(mesh):
    return jax.shard_map(
        functools.partial(on_device, mesh.shape["lat"], mesh.shape["lon"]),
        mesh=mesh,
        in_specs=(
            P(None, None, "lat", "lon"),
            P("lat", "lon", None),
            P("lat", "lon"),
            P("lat", "lon", None),
            P("lat", "lon", None),
        ),
        out_specs=(P(None, None, "lat", "lon"), P()),
        check_vma=False,
    )
```

```python
import functools
import math

import jax
import jax.numpy as jnp
from jax import lax
from jax.experimental import pallas as pl
from jax.experimental.pallas import tpu as pltpu
from jax.sharding import PartitionSpec as P

SUBSTEPS = 4

time_step = 0.15
coriolis_scale = 0.5
grav_low = 0.5
depth_top = 4.0
depth_low = 6.0
forget = 0.9
highest = lax.Precision.HIGHEST
MESH = pl.DeviceIdType.MESH

SYS = 32
BATCH = 4


def split2(x):
    high = x.astype(jnp.bfloat16)
    low = (x - high.astype(jnp.float32)).astype(jnp.bfloat16)
    return high, low


def split3(x):
    high = x.astype(jnp.bfloat16)
    rest = x - high.astype(jnp.float32)
    mid = rest.astype(jnp.bfloat16)
    low = (rest - mid.astype(jnp.float32)).astype(jnp.bfloat16)
    return high, mid, low


def dot(a, b):
    return jnp.dot(a, b, preferred_element_type=jnp.float32)


def dot_nt(a, b, precision=None):
    return lax.dot_general(
        a, b, (((1,), (1,)), ((), ())), precision=precision, preferred_element_type=jnp.float32
    )


def kernel(
    dims, x_hbm, index_hbm, count_hbm, value_hbm, weight_hbm,
    out_ref, spread_ref,
    index_ref, count_ref, value_ref, weight_ref,
    state, send_low, send_high, send_cols, from_north, from_south, from_east, from_west,
    surface, selector, means, modes, parts,
    obs_lon, obs_lat, gram_lon, gram_lat, load_sem, halo_send, halo_recv,
    obs_lon_send, obs_lon_recv, obs_lat_send, obs_lat_recv,
    gram_lon_send, gram_lon_recv, gram_lat_send, gram_lat_recv,
):
    members, fields, rows, cols, n_lat, n_lon = dims
    dirs = members - 1
    tiles = members * fields
    cells = rows * cols
    slots = index_ref.shape[1]
    me_lon, me_lat = lax.axis_index("lon"), lax.axis_index("lat")

    def lon_at(d):
        return (lax.rem(me_lon + d + n_lon, n_lon), me_lat)

    def lat_at(d):
        return (me_lon, lax.rem(me_lat + d + n_lat, n_lat))

    partners = [lon_at(d) for d in range(1, n_lon)] + [lat_at(d) for d in range(1, n_lat)]
    barrier = pltpu.get_barrier_semaphore()
    for partner in partners:
        pl.semaphore_signal(barrier, inc=1, device_id=partner, device_id_type=MESH)

    loads = [
        pltpu.make_async_copy(source, target, load_sem.at[number])
        for number, (source, target) in enumerate((
            (x_hbm, state.at[0]),
            (index_hbm, index_ref),
            (count_hbm, count_ref),
            (value_hbm, value_ref),
            (weight_hbm, weight_ref),
        ))
    ]
    for load in loads:
        load.start()

    @pl.when(me_lat == n_lat - 1)
    def _():
        from_north[...] = jnp.zeros_like(from_north)

    @pl.when(me_lat == 0)
    def _():
        from_south[...] = jnp.zeros_like(from_south)

    surface[...] = jnp.zeros_like(surface)
    lane = lax.broadcasted_iota(jnp.int32, (rows, cols), 1)
    row = lax.broadcasted_iota(jnp.int32, (rows, cols), 0)
    half = lane // 2
    first_lane, last_lane = lane == 0, lane == cols - 1
    first_row, last_row = row == 0, row == rows - 1
    even_lane = (lane - 2 * half) == 0
    edge_lane = first_lane | last_lane
    row_number = (row + me_lat * rows).astype(jnp.float32)
    coriolis = coriolis_scale * (2.0 * (row_number + 0.5) / (rows * n_lat) - 1.0)
    turn = time_step * coriolis
    ghost = 0.5 * time_step

    def put_edges(slot, now):
        for field in range(fields):
            packed = jnp.zeros((rows, cols), jnp.float32)
            for member in range(members):
                at = (member * fields + field) * rows
                moved = pltpu.roll(state[now, at : at + rows, :], 2 * member + 1, 1)
                packed = jnp.where(half == member, moved, packed)
            send_cols[slot, field * rows : (field + 1) * rows, :] = packed
        exchange_start(slot, "lon")
        for tile in range(tiles):
            send_low[slot, tile : tile + 1, :] = state[now, tile * rows : tile * rows + 1, :]
            last = (tile + 1) * rows - 1
            send_high[slot, tile : tile + 1, :] = state[now, last : last + 1, :]
        exchange_start(slot, "lat")

    def halo_copy(step, number):
        source, target, device = (
            (send_low, from_north, lat_at(-1)),
            (send_high, from_south, lat_at(1)),
            (send_cols, from_east, lon_at(-1)),
            (send_cols, from_west, lon_at(1)),
        )[number]
        return pltpu.make_async_remote_copy(
            src_ref=source.at[step],
            dst_ref=target.at[step],
            send_sem=halo_send.at[step, number],
            recv_sem=halo_recv.at[step, number],
            device_id=device,
            device_id_type=MESH,
        )

    def exchange_start(step, axis):
        if axis == "lon":
            halo_copy(step, 2).start()
            halo_copy(step, 3).start()
            return

        @pl.when(me_lat > 0)
        def _():
            halo_copy(step, 0).start()

        @pl.when(me_lat < n_lat - 1)
        def _():
            halo_copy(step, 1).start()

    def exchange_end(step, axis):
        if axis == "lon":
            halo_copy(step, 2).wait()
            halo_copy(step, 3).wait()
            return

        @pl.when(me_lat > 0)
        def _():
            halo_copy(step, 0).wait_send()
            halo_copy(step, 1).wait_recv()

        @pl.when(me_lat < n_lat - 1)
        def _():
            halo_copy(step, 1).wait_send()
            halo_copy(step, 0).wait_recv()

    for load in loads:
        load.wait()
    pl.semaphore_wait(barrier, len(partners))
    put_edges(0, 0)

    for r in range(rows):
        cell = lax.broadcasted_iota(jnp.int32, (cols, slots), 0) + r * cols
        hit = jnp.where(cell == index_ref[...], 1.0, 0.0)
        selector[r * cols : (r + 1) * cols, :] = hit.astype(jnp.bfloat16)
    live = lax.broadcasted_iota(jnp.int32, (1, slots), 1) < count_ref[...]
    weight = jnp.where(live, weight_ref[...], 0.0) / (slots * n_lat * n_lon)

    def halo_terms(halo, edge, across, side):
        pressure = halo[0] + halo[3]
        terms = []
        for layer, depth in enumerate((depth_top, depth_low)):
            h, u, v = halo[3 * layer : 3 * layer + 3]
            speed = edge[3 * layer + across]
            slope = [(depth + h) * (u, v)[across - 1], speed * u, speed * v]
            slope[across] = slope[across] + pressure
            terms += [0.25 * q - side * d for q, d in zip((h, u, v), slope)]
            pressure = pressure + grav_low * halo[3]
        return terms

    def substep(step, carry):
        now, later = lax.rem(step, 2), lax.rem(step + 1, 2)
        for member in range(members):
            here, east, west, north, south = [], [], [], [], []
            for field in range(fields):
                tile = member * fields + field
                q = state[now, tile * rows : (tile + 1) * rows, :]
                here.append(q)
                east.append(jnp.where(last_lane, 0.0, pltpu.roll(q, cols - 1, 1)))
                west.append(jnp.where(first_lane, 0.0, pltpu.roll(q, 1, 1)))
                north.append(jnp.where(last_row, 0.0, pltpu.roll(q, rows - 1, 0)))
                south.append(jnp.where(first_row, 0.0, pltpu.roll(q, 1, 0)))
            dx = [e - w for e, w in zip(east, west)]
            dy = [n - s for n, s in zip(north, south)]
            mean = [0.25 * ((e + w) + (n + s)) for e, w, n, s in zip(east, west, north, south)]
            px_top, py_top = dx[0] + dx[3], dy[0] + dy[3]
            px = (px_top, px_top + grav_low * dx[3])
            py = (py_top, py_top + grav_low * dy[3])
            after = []
            for layer, depth in enumerate((depth_top, depth_low)):
                h, u, v = 3 * layer, 3 * layer + 1, 3 * layer + 2
                flux = ((depth + east[h]) * east[u] - (depth + west[h]) * west[u]) + (
                    (depth + north[h]) * north[v] - (depth + south[h]) * south[v]
                )
                after.append(mean[h] - ghost * flux)
                after.append(
                    mean[u]
                    - ghost * (here[u] * dx[u] + here[v] * dy[u] + px[layer])
                    + turn * here[v]
                )
                after.append(
                    mean[v]
                    - ghost * (here[u] * dx[v] + here[v] * dy[v] + py[layer])
                    - turn * here[u]
                )
            for field in range(fields):
                tile = member * fields + field
                state[later, tile * rows : (tile + 1) * rows, :] = after[field]

        exchange_end(step, "lon")
        halo, edge = [], []
        for field in range(fields):
            block = slice(field * rows, (field + 1) * rows)
            from_e = pltpu.roll(from_east[step, block, :], cols - 1, 1)
            from_w = pltpu.roll(from_west[step, block, :], 1, 1)
            halo.append(jnp.where(even_lane, from_e, from_w))
            edge.append(send_cols[step, block, :])
        side = jnp.where(even_lane, ghost, -ghost)
        for field, added in enumerate(halo_terms(halo, edge, 1, side)):
            for member in range(members):
                at = (member * fields + field) * rows
                moved = pltpu.roll(added, cols - 1 - 2 * member, 1)
                state[later, at : at + rows, :] += jnp.where(edge_lane, moved, 0.0)

        exchange_end(step, "lat")
        for source, sent, at_row, side in (
            (from_north, send_high, rows - 1, ghost),
            (from_south, send_low, 0, -ghost),
        ):
            halo = [source[step, pl.ds(f, members, stride=fields), :] for f in range(fields)]
            edge = [sent[step, pl.ds(f, members, stride=fields), :] for f in range(fields)]
            for field, added in enumerate(halo_terms(halo, edge, 2, side)):
                place = pl.ds(field * rows + at_row, members, stride=fields * rows)
                state[later, place, :] = state[later, place, :] + added

        @pl.when(step + 1 < SUBSTEPS)
        def _():
            put_edges(step + 1, later)

        return carry

    lax.fori_loop(0, SUBSTEPS, substep, 0)
    final = SUBSTEPS % 2

    def gather(buffer, me, count, device_of, send, recv):
        copies = []
        for d in range(1, count):
            copy = pltpu.make_async_remote_copy(
                src_ref=buffer.at[me],
                dst_ref=buffer.at[me],
                send_sem=send.at[d],
                recv_sem=recv.at[me],
                device_id=device_of(d),
                device_id_type=MESH,
            )
            copy.start()
            copies.append(copy)

        def total():
            for d in range(1, count):
                other = lax.rem(me + d, count)
                pltpu.make_async_remote_copy(
                    src_ref=buffer.at[other],
                    dst_ref=buffer.at[other],
                    send_sem=send.at[d],
                    recv_sem=recv.at[other],
                    device_id=device_of(d),
                    device_id_type=MESH,
                ).wait_recv()
            for copy in copies:
                copy.wait_send()
            result = buffer[0]
            for i in range(1, count):
                result = result + buffer[i]
            return result

        return total

    pad = surface.shape[0]
    observed = jnp.zeros((3 * pad, slots), jnp.float32)
    for r in range(rows):
        block = slice(r * cols, (r + 1) * cols)
        surface[0:members, block] = (
            state[final, pl.ds(r, members, stride=fields * rows), :]
            + state[final, pl.ds(3 * rows + r, members, stride=fields * rows), :]
        )
        level = jnp.concatenate(split3(surface[:, block]), axis=0)
        observed += dot(level, selector[block, :])
    observed = observed[0:pad] + observed[pad : 2 * pad] + observed[2 * pad : 3 * pad]
    obs_mean = jnp.sum(observed, axis=0, keepdims=True) * (1.0 / members)
    anomaly = observed[0:dirs] - obs_mean
    innovation = value_ref[...] - obs_mean
    top = lax.broadcasted_iota(jnp.int32, (8, slots), 0) == 0
    right = jnp.concatenate(
        [jnp.zeros((SYS, slots), jnp.float32), anomaly, jnp.where(top, innovation, 0.0)], axis=0
    )
    obs_lon[me_lon] = jnp.zeros(obs_lon.shape[1:], jnp.float32)
    obs_lon[me_lon, :, 0 : right.shape[0]] = dot_nt(anomaly * weight, right, highest)
    obs_on_lon = gather(obs_lon, me_lon, n_lon, lon_at, obs_lon_send, obs_lon_recv)

    for field in range(fields):
        total = state[final, field * rows : (field + 1) * rows, :]
        for member in range(1, members):
            at = (member * fields + field) * rows
            total = total + state[final, at : at + rows, :]
        total = total * (1.0 / members)
        means[field * rows : (field + 1) * rows, :] = total
        for member in range(dirs):
            at = (member * fields + field) * rows
            modes[at : at + rows, :] = state[final, at : at + rows, :] - total
    for line in range(fields * rows):
        high, low = split2(modes[pl.ds(line, dirs, stride=fields * rows), :])
        parts[0:dirs, line * cols : (line + 1) * cols] = high
        parts[dirs : 2 * dirs, line * cols : (line + 1) * cols] = low
    high, low = parts[0:dirs, :], parts[dirs : 2 * dirs, :]
    gram_lon[me_lon] = jnp.zeros(gram_lon.shape[1:], jnp.float32)
    gram_lon[me_lon, :, 0:dirs] = dot_nt(high, high) + dot_nt(high, low) + dot_nt(low, high)
    gram_on_lon = gather(gram_lon, me_lon, n_lon, lon_at, gram_lon_send, gram_lon_recv)

    obs_lat[me_lat] = obs_on_lon()
    obs_on_lat = gather(obs_lat, me_lat, n_lat, lat_at, obs_lat_send, obs_lat_recv)
    gram_lat[me_lat] = gram_on_lon()
    gram_on_lat = gather(gram_lat, me_lat, n_lat, lat_at, gram_lat_send, gram_lat_recv)

    below = lax.broadcasted_iota(jnp.int32, (dirs, 128), 0)
    across = lax.broadcasted_iota(jnp.int32, (dirs, 128), 1)
    identity = jnp.where(across == below, 1.0, 0.0)
    inside = (across >= SYS) & (across < SYS + dirs)
    gamma = jnp.where(across == below + SYS, 1.0, 0.0) - jnp.where(inside, 1.0 / members, 0.0)
    system = obs_on_lat() + (identity + dirs / forget * gamma)
    for start in range(0, dirs, BATCH):
        batch = [
            jnp.broadcast_to(system[:, SYS + j : SYS + j + 1], system.shape)
            for j in range(start, start + BATCH)
        ]
        for i in range(BATCH):
            j = start + i
            factor = jnp.where(below > j, batch[i] * (1.0 / batch[i][j : j + 1, :]), 0.0)
            for k in range(i + 1, BATCH):
                batch[k] = batch[k] - factor * batch[k][j : j + 1, :]
            system = system - factor * system[j : j + 1, :]
    diagonal = jnp.sum(jnp.where(across == below + SYS, system, 0.0), axis=1, keepdims=True)
    system = system / jnp.sqrt(diagonal)
    solved = system[:, SYS + dirs : SYS + dirs + 1]
    inverse = system[:, 0:dirs]
    weights = jnp.sum(solved * inverse, axis=0, keepdims=True)
    shift = (math.sqrt(members) - 1.0) / dirs
    body = (shift - 1.0) / members
    tail = -math.sqrt(members) / members
    place = lax.broadcasted_iota(jnp.int32, (members, dirs), 0)
    mode = lax.broadcasted_iota(jnp.int32, (members, dirs), 1)
    omega = jnp.where(place == dirs, tail, jnp.where(place == mode, 1.0 + body, body))
    rotation = jnp.dot(
        math.sqrt(dirs) * omega, inverse, precision=highest, preferred_element_type=jnp.float32
    )
    c_high, c_low = split2(rotation + weights)
    for field in range(fields):
        block = pl.ds(field * cells, cells)
        high = parts[0:dirs, block]
        update = dot(c_high, high) + dot(c_high, parts[dirs : 2 * dirs, block]) + dot(c_low, high)
        for r in range(rows):
            line = field * rows + r
            out_ref[pl.ds(line, members, stride=fields * rows), :] = (
                update[:, r * cols : (r + 1) * cols] + means[line : line + 1, :]
            )

    mode_gram = gram_on_lat()[:, 0:dirs]
    spread = dot_nt(
        jnp.dot(rotation, mode_gram, precision=highest, preferred_element_type=jnp.float32),
        rotation,
        highest,
    )
    spread_ref[...] = spread * (1.0 / (fields * cells * n_lat * n_lon))


def on_device(n_lat, n_lon, sample_collection, obs_index, obs_count, obs_value, obs_weight):
    members, fields, rows, cols = sample_collection.shape
    slots = obs_index.shape[-1]
    dirs, tiles = members - 1, members * fields
    padded_tiles = -(-tiles // 8) * 8
    pad = -(-members // 16) * 16
    f32 = jnp.float32
    dims = (members, fields, rows, cols, n_lat, n_lon)
    analysis, spread = pl.pallas_call(
        functools.partial(kernel, dims),
        out_shape=(
            jax.ShapeDtypeStruct((tiles * rows, cols), f32),
            jax.ShapeDtypeStruct((members, members), f32),
        ),
        in_specs=[pl.BlockSpec(memory_space=pltpu.HBM)] * 5,
        out_specs=(pl.BlockSpec(memory_space=pltpu.VMEM),) * 2,
        scratch_shapes=[
            pltpu.VMEM((1, slots), jnp.int32),
            pltpu.VMEM((1, 1), jnp.int32),
            pltpu.VMEM((1, slots), f32),
            pltpu.VMEM((1, slots), f32),
            pltpu.VMEM((2, tiles * rows, cols), f32),
            pltpu.VMEM((SUBSTEPS, padded_tiles, cols), f32),
            pltpu.VMEM((SUBSTEPS, padded_tiles, cols), f32),
            pltpu.VMEM((SUBSTEPS, fields * rows, cols), f32),
            pltpu.VMEM((SUBSTEPS, padded_tiles, cols), f32),
            pltpu.VMEM((SUBSTEPS, padded_tiles, cols), f32),
            pltpu.VMEM((SUBSTEPS, fields * rows, cols), f32),
            pltpu.VMEM((SUBSTEPS, fields * rows, cols), f32),
            pltpu.VMEM((pad, rows * cols), f32),
            pltpu.VMEM((rows * cols, slots), jnp.bfloat16),
            pltpu.VMEM((fields * rows, cols), f32),
            pltpu.VMEM((dirs * fields * rows, cols), f32),
            pltpu.VMEM((2 * dirs, fields * rows * cols), jnp.bfloat16),
            pltpu.VMEM((n_lon, dirs, 128), f32),
            pltpu.VMEM((n_lat, dirs, 128), f32),
            pltpu.VMEM((n_lon, dirs, 128), f32),
            pltpu.VMEM((n_lat, dirs, 128), f32),
            pltpu.SemaphoreType.DMA((5,)),
            pltpu.SemaphoreType.DMA((SUBSTEPS, 4)),
            pltpu.SemaphoreType.DMA((SUBSTEPS, 4)),
        ]
        + [pltpu.SemaphoreType.DMA((n,)) for n in (n_lon, n_lon, n_lat, n_lat) * 2],
        compiler_params=pltpu.CompilerParams(
            collective_id=0, has_side_effects=True, vmem_limit_bytes=32 * 1024 * 1024
        ),
    )(
        sample_collection.reshape(tiles * rows, cols),
        obs_index.reshape(1, slots),
        obs_count.reshape(1, 1),
        obs_value.reshape(1, slots),
        obs_weight.reshape(1, slots),
    )
    return analysis.reshape(sample_collection.shape), spread


def solution(mesh):
    return jax.shard_map(
        functools.partial(on_device, mesh.shape["lat"], mesh.shape["lon"]),
        mesh=mesh,
        in_specs=(
            P(None, None, "lat", "lon"),
            P("lat", "lon", None),
            P("lat", "lon"),
            P("lat", "lon", None),
            P("lat", "lon", None),
        ),
        out_specs=(P(None, None, "lat", "lon"), P()),
        check_vma=False,
    )
```

```python
import functools
import math

import jax
import jax.numpy as jnp
from jax import lax
from jax.experimental import pallas as pl
from jax.experimental.pallas import tpu as pltpu
from jax.sharding import PartitionSpec as P

SUBSTEPS = 4

time_step = 0.15
coriolis_scale = 0.5
grav_low = 0.5
depth_top = 4.0
depth_low = 6.0
forget = 0.9
highest = lax.Precision.HIGHEST
MESH = pl.DeviceIdType.MESH

SYS = 32
BATCH = 4
GROUPS = 2


def split2(x):
    high = x.astype(jnp.bfloat16)
    low = (x - high.astype(jnp.float32)).astype(jnp.bfloat16)
    return high, low


def split3(x):
    high = x.astype(jnp.bfloat16)
    rest = x - high.astype(jnp.float32)
    mid = rest.astype(jnp.bfloat16)
    low = (rest - mid.astype(jnp.float32)).astype(jnp.bfloat16)
    return high, mid, low


def dot(a, b):
    return jnp.dot(a, b, preferred_element_type=jnp.float32)


def dot_nt(a, b, precision=None):
    return lax.dot_general(
        a, b, (((1,), (1,)), ((), ())), precision=precision, preferred_element_type=jnp.float32
    )


def kernel(
    dims, x_hbm, index_hbm, count_hbm, value_hbm, weight_hbm,
    out_ref, spread_ref,
    index_ref, count_ref, value_ref, weight_ref,
    state, send_low, send_high, send_cols, from_north, from_south, from_east, from_west,
    surface, selector, means, modes, parts,
    obs_lon, obs_lat, gram_lon, gram_lat, load_sem, halo_send, halo_recv,
    obs_lon_send, obs_lon_recv, obs_lat_send, obs_lat_recv,
    gram_lon_send, gram_lon_recv, gram_lat_send, gram_lat_recv,
):
    members, fields, rows, cols, n_lat, n_lon = dims
    dirs = members - 1
    tiles = members * fields
    cells = rows * cols
    slots = index_ref.shape[1]
    me_lon, me_lat = lax.axis_index("lon"), lax.axis_index("lat")

    def lon_at(d):
        return (lax.rem(me_lon + d + n_lon, n_lon), me_lat)

    def lat_at(d):
        return (me_lon, lax.rem(me_lat + d + n_lat, n_lat))

    partners = [lon_at(d) for d in range(1, n_lon)] + [lat_at(d) for d in range(1, n_lat)]
    barrier = pltpu.get_barrier_semaphore()
    for partner in partners:
        pl.semaphore_signal(barrier, inc=1, device_id=partner, device_id_type=MESH)

    loads = [
        pltpu.make_async_copy(source, target, load_sem.at[number])
        for number, (source, target) in enumerate((
            (x_hbm, state.at[0]),
            (index_hbm, index_ref),
            (count_hbm, count_ref),
            (value_hbm, value_ref),
            (weight_hbm, weight_ref),
        ))
    ]
    for load in loads:
        load.start()

    @pl.when(me_lat == n_lat - 1)
    def _():
        from_north[...] = jnp.zeros_like(from_north)

    @pl.when(me_lat == 0)
    def _():
        from_south[...] = jnp.zeros_like(from_south)

    surface[...] = jnp.zeros_like(surface)
    lane = lax.broadcasted_iota(jnp.int32, (rows, cols), 1)
    row = lax.broadcasted_iota(jnp.int32, (rows, cols), 0)
    half = lane // 2
    first_lane, last_lane = lane == 0, lane == cols - 1
    first_row, last_row = row == 0, row == rows - 1
    even_lane = (lane - 2 * half) == 0
    edge_lane = first_lane | last_lane
    row_number = (row + me_lat * rows).astype(jnp.float32)
    coriolis = coriolis_scale * (2.0 * (row_number + 0.5) / (rows * n_lat) - 1.0)
    turn = time_step * coriolis
    ghost = 0.5 * time_step

    bounds = [members * g // GROUPS for g in range(GROUPS + 1)]

    def put_edges(slot, group, now):
        first, last = bounds[group], bounds[group + 1]
        for field in range(fields):
            packed = jnp.zeros((rows, cols), jnp.float32)
            for member in range(first, last):
                at = (member * fields + field) * rows
                moved = pltpu.roll(state[now, at : at + rows, :], 2 * (member - first) + 1, 1)
                packed = jnp.where(half == member - first, moved, packed)
            send_cols[slot, group, field * rows : (field + 1) * rows, :] = packed
        exchange_start(slot, group, "lon")
        for tile in range(first * fields, last * fields):
            place = slice(tile - first * fields, tile - first * fields + 1)
            low, high = tile * rows, (tile + 1) * rows - 1
            send_low[slot, group, place, :] = state[now, low : low + 1, :]
            send_high[slot, group, place, :] = state[now, high : high + 1, :]
        exchange_start(slot, group, "lat")

    def halo_copy(step, group, number):
        source, target, device = (
            (send_low, from_north, lat_at(-1)),
            (send_high, from_south, lat_at(1)),
            (send_cols, from_east, lon_at(-1)),
            (send_cols, from_west, lon_at(1)),
        )[number]
        return pltpu.make_async_remote_copy(
            src_ref=source.at[step, group],
            dst_ref=target.at[step, group],
            send_sem=halo_send.at[step, group, number],
            recv_sem=halo_recv.at[step, group, number],
            device_id=device,
            device_id_type=MESH,
        )

    def exchange_start(step, group, axis):
        if axis == "lon":
            halo_copy(step, group, 2).start()
            halo_copy(step, group, 3).start()
            return

        @pl.when(me_lat > 0)
        def _():
            halo_copy(step, group, 0).start()

        @pl.when(me_lat < n_lat - 1)
        def _():
            halo_copy(step, group, 1).start()

    def exchange_end(step, group, axis):
        if axis == "lon":
            halo_copy(step, group, 2).wait()
            halo_copy(step, group, 3).wait()
            return

        @pl.when(me_lat > 0)
        def _():
            halo_copy(step, group, 0).wait_send()
            halo_copy(step, group, 1).wait_recv()

        @pl.when(me_lat < n_lat - 1)
        def _():
            halo_copy(step, group, 1).wait_send()
            halo_copy(step, group, 0).wait_recv()

    for load in loads:
        load.wait()
    pl.semaphore_wait(barrier, len(partners))
    for group in range(GROUPS):
        put_edges(0, group, 0)

    for r in range(rows):
        cell = lax.broadcasted_iota(jnp.int32, (cols, slots), 0) + r * cols
        hit = jnp.where(cell == index_ref[...], 1.0, 0.0)
        selector[r * cols : (r + 1) * cols, :] = hit.astype(jnp.bfloat16)
    live = lax.broadcasted_iota(jnp.int32, (1, slots), 1) < count_ref[...]
    weight = jnp.where(live, weight_ref[...], 0.0) / (slots * n_lat * n_lon)

    def halo_terms(halo, edge, across, side):
        pressure = halo[0] + halo[3]
        terms = []
        for layer, depth in enumerate((depth_top, depth_low)):
            h, u, v = halo[3 * layer : 3 * layer + 3]
            speed = edge[3 * layer + across]
            slope = [(depth + h) * (u, v)[across - 1], speed * u, speed * v]
            slope[across] = slope[across] + pressure
            terms += [0.25 * q - side * d for q, d in zip((h, u, v), slope)]
            pressure = pressure + grav_low * halo[3]
        return terms

    def finish(step, group, later):
        first, last = bounds[group], bounds[group + 1]
        exchange_end(step, group, "lon")
        halo, edge = [], []
        for field in range(fields):
            block = slice(field * rows, (field + 1) * rows)
            from_e = pltpu.roll(from_east[step, group, block, :], cols - 1, 1)
            from_w = pltpu.roll(from_west[step, group, block, :], 1, 1)
            halo.append(jnp.where(even_lane, from_e, from_w))
            edge.append(send_cols[step, group, block, :])
        side = jnp.where(even_lane, ghost, -ghost)
        for field, added in enumerate(halo_terms(halo, edge, 1, side)):
            for member in range(first, last):
                at = (member * fields + field) * rows
                moved = pltpu.roll(added, cols - 1 - 2 * (member - first), 1)
                state[later, at : at + rows, :] += jnp.where(edge_lane, moved, 0.0)

        exchange_end(step, group, "lat")
        for source, sent, at_row, side in (
            (from_north, send_high, rows - 1, ghost),
            (from_south, send_low, 0, -ghost),
        ):
            lines = [pl.ds(field, last - first, stride=fields) for field in range(fields)]
            halo = [source[step, group, line, :] for line in lines]
            edge = [sent[step, group, line, :] for line in lines]
            for field, added in enumerate(halo_terms(halo, edge, 2, side)):
                at = (first * fields + field) * rows + at_row
                place = pl.ds(at, last - first, stride=fields * rows)
                state[later, place, :] = state[later, place, :] + added

        @pl.when(step + 1 < SUBSTEPS)
        def _():
            put_edges(step + 1, group, later)

    def substep(step, carry):
        now, later = lax.rem(step, 2), lax.rem(step + 1, 2)
        for member in range(members):
            here, east, west, north, south = [], [], [], [], []
            for field in range(fields):
                tile = member * fields + field
                q = state[now, tile * rows : (tile + 1) * rows, :]
                here.append(q)
                east.append(jnp.where(last_lane, 0.0, pltpu.roll(q, cols - 1, 1)))
                west.append(jnp.where(first_lane, 0.0, pltpu.roll(q, 1, 1)))
                north.append(jnp.where(last_row, 0.0, pltpu.roll(q, rows - 1, 0)))
                south.append(jnp.where(first_row, 0.0, pltpu.roll(q, 1, 0)))
            dx = [e - w for e, w in zip(east, west)]
            dy = [n - s for n, s in zip(north, south)]
            mean = [0.25 * ((e + w) + (n + s)) for e, w, n, s in zip(east, west, north, south)]
            px_top, py_top = dx[0] + dx[3], dy[0] + dy[3]
            px = (px_top, px_top + grav_low * dx[3])
            py = (py_top, py_top + grav_low * dy[3])
            after = []
            for layer, depth in enumerate((depth_top, depth_low)):
                h, u, v = 3 * layer, 3 * layer + 1, 3 * layer + 2
                flux = ((depth + east[h]) * east[u] - (depth + west[h]) * west[u]) + (
                    (depth + north[h]) * north[v] - (depth + south[h]) * south[v]
                )
                after.append(mean[h] - ghost * flux)
                after.append(
                    mean[u]
                    - ghost * (here[u] * dx[u] + here[v] * dy[u] + px[layer])
                    + turn * here[v]
                )
                after.append(
                    mean[v]
                    - ghost * (here[u] * dx[v] + here[v] * dy[v] + py[layer])
                    - turn * here[u]
                )
            for field in range(fields):
                tile = member * fields + field
                state[later, tile * rows : (tile + 1) * rows, :] = after[field]

        for group in range(GROUPS):
            finish(step, group, later)
        return carry

    lax.fori_loop(0, SUBSTEPS, substep, 0)
    final = SUBSTEPS % 2

    def gather(buffer, me, count, device_of, send, recv):
        copies = []
        for d in range(1, count):
            copy = pltpu.make_async_remote_copy(
                src_ref=buffer.at[me],
                dst_ref=buffer.at[me],
                send_sem=send.at[d],
                recv_sem=recv.at[me],
                device_id=device_of(d),
                device_id_type=MESH,
            )
            copy.start()
            copies.append(copy)

        def total():
            for d in range(1, count):
                other = lax.rem(me + d, count)
                pltpu.make_async_remote_copy(
                    src_ref=buffer.at[other],
                    dst_ref=buffer.at[other],
                    send_sem=send.at[d],
                    recv_sem=recv.at[other],
                    device_id=device_of(d),
                    device_id_type=MESH,
                ).wait_recv()
            for copy in copies:
                copy.wait_send()
            result = buffer[0]
            for i in range(1, count):
                result = result + buffer[i]
            return result

        return total

    pad = surface.shape[0]
    observed = jnp.zeros((3 * pad, slots), jnp.float32)
    for r in range(rows):
        block = slice(r * cols, (r + 1) * cols)
        surface[0:members, block] = (
            state[final, pl.ds(r, members, stride=fields * rows), :]
            + state[final, pl.ds(3 * rows + r, members, stride=fields * rows), :]
        )
        level = jnp.concatenate(split3(surface[:, block]), axis=0)
        observed += dot(level, selector[block, :])
    observed = observed[0:pad] + observed[pad : 2 * pad] + observed[2 * pad : 3 * pad]
    obs_mean = jnp.sum(observed, axis=0, keepdims=True) * (1.0 / members)
    anomaly = observed[0:dirs] - obs_mean
    innovation = value_ref[...] - obs_mean
    top = lax.broadcasted_iota(jnp.int32, (8, slots), 0) == 0
    right = jnp.concatenate(
        [jnp.zeros((SYS, slots), jnp.float32), anomaly, jnp.where(top, innovation, 0.0)], axis=0
    )
    obs_lon[me_lon] = jnp.zeros(obs_lon.shape[1:], jnp.float32)
    obs_lon[me_lon, :, 0 : right.shape[0]] = dot_nt(anomaly * weight, right, highest)
    obs_on_lon = gather(obs_lon, me_lon, n_lon, lon_at, obs_lon_send, obs_lon_recv)

    for field in range(fields):
        total = state[final, field * rows : (field + 1) * rows, :]
        for member in range(1, members):
            at = (member * fields + field) * rows
            total = total + state[final, at : at + rows, :]
        total = total * (1.0 / members)
        means[field * rows : (field + 1) * rows, :] = total
        for member in range(dirs):
            at = (member * fields + field) * rows
            modes[at : at + rows, :] = state[final, at : at + rows, :] - total
    for line in range(fields * rows):
        high, low = split2(modes[pl.ds(line, dirs, stride=fields * rows), :])
        parts[0:dirs, line * cols : (line + 1) * cols] = high
        parts[dirs : 2 * dirs, line * cols : (line + 1) * cols] = low
    high, low = parts[0:dirs, :], parts[dirs : 2 * dirs, :]
    gram_lon[me_lon] = jnp.zeros(gram_lon.shape[1:], jnp.float32)
    gram_lon[me_lon, :, 0:dirs] = dot_nt(high, high) + dot_nt(high, low) + dot_nt(low, high)
    gram_on_lon = gather(gram_lon, me_lon, n_lon, lon_at, gram_lon_send, gram_lon_recv)

    obs_lat[me_lat] = obs_on_lon()
    obs_on_lat = gather(obs_lat, me_lat, n_lat, lat_at, obs_lat_send, obs_lat_recv)
    gram_lat[me_lat] = gram_on_lon()
    gram_on_lat = gather(gram_lat, me_lat, n_lat, lat_at, gram_lat_send, gram_lat_recv)

    below = lax.broadcasted_iota(jnp.int32, (dirs, 128), 0)
    across = lax.broadcasted_iota(jnp.int32, (dirs, 128), 1)
    identity = jnp.where(across == below, 1.0, 0.0)
    inside = (across >= SYS) & (across < SYS + dirs)
    gamma = jnp.where(across == below + SYS, 1.0, 0.0) - jnp.where(inside, 1.0 / members, 0.0)
    system = obs_on_lat() + (identity + dirs / forget * gamma)
    for start in range(0, dirs, BATCH):
        batch = [
            jnp.broadcast_to(system[:, SYS + j : SYS + j + 1], system.shape)
            for j in range(start, start + BATCH)
        ]
        for i in range(BATCH):
            j = start + i
            factor = jnp.where(below > j, batch[i] * (1.0 / batch[i][j : j + 1, :]), 0.0)
            for k in range(i + 1, BATCH):
                batch[k] = batch[k] - factor * batch[k][j : j + 1, :]
            system = system - factor * system[j : j + 1, :]
    diagonal = jnp.sum(jnp.where(across == below + SYS, system, 0.0), axis=1, keepdims=True)
    system = system / jnp.sqrt(diagonal)
    solved = system[:, SYS + dirs : SYS + dirs + 1]
    inverse = system[:, 0:dirs]
    weights = jnp.sum(solved * inverse, axis=0, keepdims=True)
    shift = (math.sqrt(members) - 1.0) / dirs
    body = (shift - 1.0) / members
    tail = -math.sqrt(members) / members
    place = lax.broadcasted_iota(jnp.int32, (members, dirs), 0)
    mode = lax.broadcasted_iota(jnp.int32, (members, dirs), 1)
    omega = jnp.where(place == dirs, tail, jnp.where(place == mode, 1.0 + body, body))
    rotation = jnp.dot(
        math.sqrt(dirs) * omega, inverse, precision=highest, preferred_element_type=jnp.float32
    )
    mode_gram = gram_on_lat()[:, 0:dirs]
    spread = dot_nt(
        jnp.dot(rotation, mode_gram, precision=highest, preferred_element_type=jnp.float32),
        rotation,
        highest,
    )
    spread_ref[...] = spread * (1.0 / (fields * cells * n_lat * n_lon))

    c_high, c_low = split2(rotation + weights)
    for field in range(fields):
        block = pl.ds(field * cells, cells)
        high = parts[0:dirs, block]
        update = dot(c_high, high) + dot(c_high, parts[dirs : 2 * dirs, block]) + dot(c_low, high)
        for r in range(rows):
            line = field * rows + r
            out_ref[pl.ds(line, members, stride=fields * rows), :] = (
                update[:, r * cols : (r + 1) * cols] + means[line : line + 1, :]
            )


def on_device(n_lat, n_lon, sample_collection, obs_index, obs_count, obs_value, obs_weight):
    members, fields, rows, cols = sample_collection.shape
    slots = obs_index.shape[-1]
    dirs, tiles = members - 1, members * fields
    group_tiles = -(-members // GROUPS) * fields
    padded_tiles = -(-group_tiles // 8) * 8
    pad = -(-members // 16) * 16
    f32 = jnp.float32
    dims = (members, fields, rows, cols, n_lat, n_lon)
    analysis, spread = pl.pallas_call(
        functools.partial(kernel, dims),
        out_shape=(
            jax.ShapeDtypeStruct((tiles * rows, cols), f32),
            jax.ShapeDtypeStruct((members, members), f32),
        ),
        in_specs=[pl.BlockSpec(memory_space=pltpu.HBM)] * 5,
        out_specs=(pl.BlockSpec(memory_space=pltpu.VMEM),) * 2,
        scratch_shapes=[
            pltpu.VMEM((1, slots), jnp.int32),
            pltpu.VMEM((1, 1), jnp.int32),
            pltpu.VMEM((1, slots), f32),
            pltpu.VMEM((1, slots), f32),
            pltpu.VMEM((2, tiles * rows, cols), f32),
            pltpu.VMEM((SUBSTEPS, GROUPS, padded_tiles, cols), f32),
            pltpu.VMEM((SUBSTEPS, GROUPS, padded_tiles, cols), f32),
            pltpu.VMEM((SUBSTEPS, GROUPS, fields * rows, cols), f32),
            pltpu.VMEM((SUBSTEPS, GROUPS, padded_tiles, cols), f32),
            pltpu.VMEM((SUBSTEPS, GROUPS, padded_tiles, cols), f32),
            pltpu.VMEM((SUBSTEPS, GROUPS, fields * rows, cols), f32),
            pltpu.VMEM((SUBSTEPS, GROUPS, fields * rows, cols), f32),
            pltpu.VMEM((pad, rows * cols), f32),
            pltpu.VMEM((rows * cols, slots), jnp.bfloat16),
            pltpu.VMEM((fields * rows, cols), f32),
            pltpu.VMEM((dirs * fields * rows, cols), f32),
            pltpu.VMEM((2 * dirs, fields * rows * cols), jnp.bfloat16),
            pltpu.VMEM((n_lon, dirs, 128), f32),
            pltpu.VMEM((n_lat, dirs, 128), f32),
            pltpu.VMEM((n_lon, dirs, 128), f32),
            pltpu.VMEM((n_lat, dirs, 128), f32),
            pltpu.SemaphoreType.DMA((5,)),
            pltpu.SemaphoreType.DMA((SUBSTEPS, GROUPS, 4)),
            pltpu.SemaphoreType.DMA((SUBSTEPS, GROUPS, 4)),
        ]
        + [pltpu.SemaphoreType.DMA((n,)) for n in (n_lon, n_lon, n_lat, n_lat) * 2],
        compiler_params=pltpu.CompilerParams(
            collective_id=0, has_side_effects=True, vmem_limit_bytes=32 * 1024 * 1024
        ),
    )(
        sample_collection.reshape(tiles * rows, cols),
        obs_index.reshape(1, slots),
        obs_count.reshape(1, 1),
        obs_value.reshape(1, slots),
        obs_weight.reshape(1, slots),
    )
    return analysis.reshape(sample_collection.shape), spread


def solution(mesh):
    return jax.shard_map(
        functools.partial(on_device, mesh.shape["lat"], mesh.shape["lon"]),
        mesh=mesh,
        in_specs=(
            P(None, None, "lat", "lon"),
            P("lat", "lon", None),
            P("lat", "lon"),
            P("lat", "lon", None),
            P("lat", "lon", None),
        ),
        out_specs=(P(None, None, "lat", "lon"), P()),
        check_vma=False,
    )
```

```python
import functools
import math

import jax
import jax.numpy as jnp
from jax import lax
from jax.experimental import pallas as pl
from jax.experimental.pallas import tpu as pltpu
from jax.sharding import PartitionSpec as P

SUBSTEPS = 4

time_step = 0.15
coriolis_scale = 0.5
grav_low = 0.5
depth_top = 4.0
depth_low = 6.0
forget = 0.9
highest = lax.Precision.HIGHEST
MESH = pl.DeviceIdType.MESH

SYS = 32
BATCH = 4
GROUPS = 2
VMEM_BYTES = 63 * 1024 * 1024


def split2(x):
    high = x.astype(jnp.bfloat16)
    low = (x - high.astype(jnp.float32)).astype(jnp.bfloat16)
    return high, low


def split3(x):
    high = x.astype(jnp.bfloat16)
    rest = x - high.astype(jnp.float32)
    mid = rest.astype(jnp.bfloat16)
    low = (rest - mid.astype(jnp.float32)).astype(jnp.bfloat16)
    return high, mid, low


def dot(a, b):
    return jnp.dot(a, b, preferred_element_type=jnp.float32)


def dot_nt(a, b, precision=None):
    return lax.dot_general(
        a, b, (((1,), (1,)), ((), ())), precision=precision, preferred_element_type=jnp.float32
    )


def kernel(
    dims, x_hbm, index_hbm, count_hbm, value_hbm, weight_hbm,
    out_hbm, spread_ref,
    index_ref, count_ref, value_ref, weight_ref,
    out_ref, state, send_low, send_high, send_cols, from_north, from_south, from_east, from_west,
    surface, selector, means, modes, parts,
    obs_lon, obs_lat, gram_lon, gram_lat, load_sem, store_sem, halo_send, halo_recv,
    obs_lon_send, obs_lon_recv, obs_lat_send, obs_lat_recv,
    gram_lon_send, gram_lon_recv, gram_lat_send, gram_lat_recv,
):
    members, fields, rows, cols, n_lat, n_lon = dims
    dirs = members - 1
    tiles = members * fields
    cells = rows * cols
    slots = index_ref.shape[1]
    me_lon, me_lat = lax.axis_index("lon"), lax.axis_index("lat")

    def lon_at(d):
        return (lax.rem(me_lon + d + n_lon, n_lon), me_lat)

    def lat_at(d):
        return (me_lon, lax.rem(me_lat + d + n_lat, n_lat))

    partners = [lon_at(d) for d in range(1, n_lon)] + [lat_at(d) for d in range(1, n_lat)]
    barrier = pltpu.get_barrier_semaphore()
    for partner in partners:
        pl.semaphore_signal(barrier, inc=1, device_id=partner, device_id_type=MESH)

    loads = [
        pltpu.make_async_copy(source, target, load_sem.at[number])
        for number, (source, target) in enumerate((
            (x_hbm, state.at[0]),
            (index_hbm, index_ref),
            (count_hbm, count_ref),
            (value_hbm, value_ref),
            (weight_hbm, weight_ref),
        ))
    ]
    for load in loads:
        load.start()

    @pl.when(me_lat == n_lat - 1)
    def _():
        from_north[...] = jnp.zeros_like(from_north)

    @pl.when(me_lat == 0)
    def _():
        from_south[...] = jnp.zeros_like(from_south)

    surface[...] = jnp.zeros_like(surface)
    lane = lax.broadcasted_iota(jnp.int32, (rows, cols), 1)
    row = lax.broadcasted_iota(jnp.int32, (rows, cols), 0)
    half = lane // 2
    first_lane, last_lane = lane == 0, lane == cols - 1
    first_row, last_row = row == 0, row == rows - 1
    even_lane = (lane - 2 * half) == 0
    edge_lane = first_lane | last_lane
    row_number = (row + me_lat * rows).astype(jnp.float32)
    coriolis = coriolis_scale * (2.0 * (row_number + 0.5) / (rows * n_lat) - 1.0)
    turn = time_step * coriolis
    ghost = 0.5 * time_step

    bounds = [members * g // GROUPS for g in range(GROUPS + 1)]

    def put_cols(slot, group, now):
        first, last = bounds[group], bounds[group + 1]
        for field in range(fields):
            packed = jnp.zeros((rows, cols), jnp.float32)
            for member in range(first, last):
                at = (member * fields + field) * rows
                moved = pltpu.roll(state[now, at : at + rows, :], 2 * (member - first) + 1, 1)
                packed = jnp.where(half == member - first, moved, packed)
            send_cols[slot, group, field * rows : (field + 1) * rows, :] = packed
        exchange_start(slot, group, "lon")

    def lines_of(group, field, at_row):
        first, count = bounds[group], bounds[group + 1] - bounds[group]
        at = (first * fields + field) * rows + at_row
        return pl.ds(at, count, stride=fields * rows), pl.ds(field, count, stride=fields)

    def halo_copy(step, group, number):
        source, target, device = (
            (send_low, from_north, lat_at(-1)),
            (send_high, from_south, lat_at(1)),
            (send_cols, from_east, lon_at(-1)),
            (send_cols, from_west, lon_at(1)),
        )[number]
        return pltpu.make_async_remote_copy(
            src_ref=source.at[step, group],
            dst_ref=target.at[step, group],
            send_sem=halo_send.at[step, group, number],
            recv_sem=halo_recv.at[step, group, number],
            device_id=device,
            device_id_type=MESH,
        )

    def exchange_start(step, group, axis):
        if axis == "lon":
            halo_copy(step, group, 2).start()
            halo_copy(step, group, 3).start()
            return

        @pl.when(me_lat > 0)
        def _():
            halo_copy(step, group, 0).start()

        @pl.when(me_lat < n_lat - 1)
        def _():
            halo_copy(step, group, 1).start()

    def exchange_end(step, group, axis):
        if axis == "lon":
            halo_copy(step, group, 2).wait()
            halo_copy(step, group, 3).wait()
            return

        @pl.when(me_lat > 0)
        def _():
            halo_copy(step, group, 0).wait_send()
            halo_copy(step, group, 1).wait_recv()

        @pl.when(me_lat < n_lat - 1)
        def _():
            halo_copy(step, group, 1).wait_send()
            halo_copy(step, group, 0).wait_recv()

    for load in loads:
        load.wait()
    pl.semaphore_wait(barrier, len(partners))
    for group in range(GROUPS):
        for sent, at_row in ((send_low, 0), (send_high, rows - 1)):
            for field in range(fields):
                place, line = lines_of(group, field, at_row)
                sent[0, group, line, :] = state[0, place, :]
        exchange_start(0, group, "lat")
        put_cols(0, group, 0)

    for r in range(rows):
        cell = lax.broadcasted_iota(jnp.int32, (cols, slots), 0) + r * cols
        hit = jnp.where(cell == index_ref[...], 1.0, 0.0)
        selector[r * cols : (r + 1) * cols, :] = hit.astype(jnp.bfloat16)
    live = lax.broadcasted_iota(jnp.int32, (1, slots), 1) < count_ref[...]
    weight = jnp.where(live, weight_ref[...], 0.0) / (slots * n_lat * n_lon)

    def halo_terms(halo, edge, across, side):
        pressure = halo[0] + halo[3]
        terms = []
        for layer, depth in enumerate((depth_top, depth_low)):
            h, u, v = halo[3 * layer : 3 * layer + 3]
            speed = edge[3 * layer + across]
            slope = [(depth + h) * (u, v)[across - 1], speed * u, speed * v]
            slope[across] = slope[across] + pressure
            terms += [0.25 * q - side * d for q, d in zip((h, u, v), slope)]
            pressure = pressure + grav_low * halo[3]
        return terms

    def finish(step, group, later):
        first, last = bounds[group], bounds[group + 1]
        exchange_end(step, group, "lon")
        halo, edge = [], []
        for field in range(fields):
            block = slice(field * rows, (field + 1) * rows)
            from_e = pltpu.roll(from_east[step, group, block, :], cols - 1, 1)
            from_w = pltpu.roll(from_west[step, group, block, :], 1, 1)
            halo.append(jnp.where(even_lane, from_e, from_w))
            edge.append(send_cols[step, group, block, :])
        side = jnp.where(even_lane, ghost, -ghost)
        for field, added in enumerate(halo_terms(halo, edge, 1, side)):
            for member in range(first, last):
                at = (member * fields + field) * rows
                moved = pltpu.roll(added, cols - 1 - 2 * (member - first), 1)
                state[later, at : at + rows, :] += jnp.where(edge_lane, moved, 0.0)

        exchange_end(step, group, "lat")
        for source, sent, at_row, side in (
            (from_north, send_high, rows - 1, ghost),
            (from_south, send_low, 0, -ghost),
        ):
            places, lines = zip(*(lines_of(group, field, at_row) for field in range(fields)))
            halo = [source[step, group, line, :] for line in lines]
            edge = [sent[step, group, line, :] for line in lines]
            for field, added in enumerate(halo_terms(halo, edge, 2, side)):
                moved = state[later, places[field], :] + added
                state[later, places[field], :] = moved
                sent[step + 1, group, lines[field], :] = moved

        @pl.when(step + 1 < SUBSTEPS)
        def _():
            exchange_start(step + 1, group, "lat")
            put_cols(step + 1, group, later)

    def substep(step, carry):
        now, later = lax.rem(step, 2), lax.rem(step + 1, 2)
        for member in range(members):
            here, east, west, north, south = [], [], [], [], []
            for field in range(fields):
                tile = member * fields + field
                q = state[now, tile * rows : (tile + 1) * rows, :]
                here.append(q)
                east.append(jnp.where(last_lane, 0.0, pltpu.roll(q, cols - 1, 1)))
                west.append(jnp.where(first_lane, 0.0, pltpu.roll(q, 1, 1)))
                north.append(jnp.where(last_row, 0.0, pltpu.roll(q, rows - 1, 0)))
                south.append(jnp.where(first_row, 0.0, pltpu.roll(q, 1, 0)))
            dx = [e - w for e, w in zip(east, west)]
            dy = [n - s for n, s in zip(north, south)]
            mean = [0.25 * ((e + w) + (n + s)) for e, w, n, s in zip(east, west, north, south)]
            px_top, py_top = dx[0] + dx[3], dy[0] + dy[3]
            px = (px_top, px_top + grav_low * dx[3])
            py = (py_top, py_top + grav_low * dy[3])
            after = []
            for layer, depth in enumerate((depth_top, depth_low)):
                h, u, v = 3 * layer, 3 * layer + 1, 3 * layer + 2
                flux = ((depth + east[h]) * east[u] - (depth + west[h]) * west[u]) + (
                    (depth + north[h]) * north[v] - (depth + south[h]) * south[v]
                )
                after.append(mean[h] - ghost * flux)
                after.append(
                    mean[u]
                    - ghost * (here[u] * dx[u] + here[v] * dy[u] + px[layer])
                    + turn * here[v]
                )
                after.append(
                    mean[v]
                    - ghost * (here[u] * dx[v] + here[v] * dy[v] + py[layer])
                    - turn * here[u]
                )
            for field in range(fields):
                tile = member * fields + field
                state[later, tile * rows : (tile + 1) * rows, :] = after[field]

        for group in range(GROUPS):
            finish(step, group, later)
        return carry

    lax.fori_loop(0, SUBSTEPS, substep, 0)
    final = SUBSTEPS % 2

    def gather(buffer, me, count, device_of, send, recv):
        copies = []
        for d in range(1, count):
            copy = pltpu.make_async_remote_copy(
                src_ref=buffer.at[me],
                dst_ref=buffer.at[me],
                send_sem=send.at[d],
                recv_sem=recv.at[me],
                device_id=device_of(d),
                device_id_type=MESH,
            )
            copy.start()
            copies.append(copy)

        def total():
            for d in range(1, count):
                other = lax.rem(me + d, count)
                pltpu.make_async_remote_copy(
                    src_ref=buffer.at[other],
                    dst_ref=buffer.at[other],
                    send_sem=send.at[d],
                    recv_sem=recv.at[other],
                    device_id=device_of(d),
                    device_id_type=MESH,
                ).wait_recv()
            for copy in copies:
                copy.wait_send()
            result = buffer[0]
            for i in range(1, count):
                result = result + buffer[i]
            return result

        return total

    pad = surface.shape[0]
    observed = jnp.zeros((3 * pad, slots), jnp.float32)
    for r in range(rows):
        block = slice(r * cols, (r + 1) * cols)
        surface[0:members, block] = (
            state[final, pl.ds(r, members, stride=fields * rows), :]
            + state[final, pl.ds(3 * rows + r, members, stride=fields * rows), :]
        )
        level = jnp.concatenate(split3(surface[:, block]), axis=0)
        observed += dot(level, selector[block, :])
    observed = observed[0:pad] + observed[pad : 2 * pad] + observed[2 * pad : 3 * pad]
    obs_mean = jnp.sum(observed, axis=0, keepdims=True) * (1.0 / members)
    anomaly = observed[0:dirs] - obs_mean
    innovation = value_ref[...] - obs_mean
    top = lax.broadcasted_iota(jnp.int32, (8, slots), 0) == 0
    right = jnp.concatenate(
        [jnp.zeros((SYS, slots), jnp.float32), anomaly, jnp.where(top, innovation, 0.0)], axis=0
    )
    obs_lon[me_lon] = jnp.zeros(obs_lon.shape[1:], jnp.float32)
    obs_lon[me_lon, :, 0 : right.shape[0]] = dot_nt(anomaly * weight, right, highest)
    obs_on_lon = gather(obs_lon, me_lon, n_lon, lon_at, obs_lon_send, obs_lon_recv)

    for field in range(fields):
        total = state[final, field * rows : (field + 1) * rows, :]
        for member in range(1, members):
            at = (member * fields + field) * rows
            total = total + state[final, at : at + rows, :]
        total = total * (1.0 / members)
        means[field * rows : (field + 1) * rows, :] = total
        for member in range(dirs):
            at = (member * fields + field) * rows
            modes[at : at + rows, :] = state[final, at : at + rows, :] - total
    for line in range(fields * rows):
        high, low = split2(modes[pl.ds(line, dirs, stride=fields * rows), :])
        parts[0:dirs, line * cols : (line + 1) * cols] = high
        parts[dirs : 2 * dirs, line * cols : (line + 1) * cols] = low
    high, low = parts[0:dirs, :], parts[dirs : 2 * dirs, :]
    gram_lon[me_lon] = jnp.zeros(gram_lon.shape[1:], jnp.float32)
    gram_lon[me_lon, :, 0:dirs] = dot_nt(high, high) + dot_nt(high, low) + dot_nt(low, high)
    gram_on_lon = gather(gram_lon, me_lon, n_lon, lon_at, gram_lon_send, gram_lon_recv)

    obs_lat[me_lat] = obs_on_lon()
    obs_on_lat = gather(obs_lat, me_lat, n_lat, lat_at, obs_lat_send, obs_lat_recv)
    gram_lat[me_lat] = gram_on_lon()
    gram_on_lat = gather(gram_lat, me_lat, n_lat, lat_at, gram_lat_send, gram_lat_recv)

    below = lax.broadcasted_iota(jnp.int32, (dirs, 128), 0)
    across = lax.broadcasted_iota(jnp.int32, (dirs, 128), 1)
    identity = jnp.where(across == below, 1.0, 0.0)
    inside = (across >= SYS) & (across < SYS + dirs)
    gamma = jnp.where(across == below + SYS, 1.0, 0.0) - jnp.where(inside, 1.0 / members, 0.0)
    system = obs_on_lat() + (identity + dirs / forget * gamma)
    for start in range(0, dirs, BATCH):
        batch = [
            jnp.broadcast_to(system[:, SYS + j : SYS + j + 1], system.shape)
            for j in range(start, start + BATCH)
        ]
        for i in range(BATCH):
            j = start + i
            factor = jnp.where(below > j, batch[i] * (1.0 / batch[i][j : j + 1, :]), 0.0)
            for k in range(i + 1, BATCH):
                batch[k] = batch[k] - factor * batch[k][j : j + 1, :]
            system = system - factor * system[j : j + 1, :]
    diagonal = jnp.sum(jnp.where(across == below + SYS, system, 0.0), axis=1, keepdims=True)
    system = system / jnp.sqrt(diagonal)
    solved = system[:, SYS + dirs : SYS + dirs + 1]
    inverse = system[:, 0:dirs]
    weights = jnp.sum(solved * inverse, axis=0, keepdims=True)
    shift = (math.sqrt(members) - 1.0) / dirs
    body = (shift - 1.0) / members
    tail = -math.sqrt(members) / members
    place = lax.broadcasted_iota(jnp.int32, (members, dirs), 0)
    mode = lax.broadcasted_iota(jnp.int32, (members, dirs), 1)
    omega = jnp.where(place == dirs, tail, jnp.where(place == mode, 1.0 + body, body))
    rotation = jnp.dot(
        math.sqrt(dirs) * omega, inverse, precision=highest, preferred_element_type=jnp.float32
    )
    mode_gram = gram_on_lat()[:, 0:dirs]
    spread = dot_nt(
        jnp.dot(rotation, mode_gram, precision=highest, preferred_element_type=jnp.float32),
        rotation,
        highest,
    )
    spread_ref[...] = spread * (1.0 / (fields * cells * n_lat * n_lon))

    stores = []
    c_high, c_low = split2(rotation + weights)
    for field in range(fields):
        block = pl.ds(field * cells, cells)
        high = parts[0:dirs, block]
        update = dot(c_high, high) + dot(c_high, parts[dirs : 2 * dirs, block]) + dot(c_low, high)
        for r in range(rows):
            line = field * rows + r
            out_ref[:, line, :] = update[:, r * cols : (r + 1) * cols] + means[line : line + 1, :]
        block = slice(field * rows, (field + 1) * rows)
        store = pltpu.make_async_copy(
            out_ref.at[:, block, :], out_hbm.at[:, block, :], store_sem.at[field]
        )
        store.start()
        stores.append(store)
    for store in stores:
        store.wait()


def on_device(n_lat, n_lon, sample_collection, obs_index, obs_count, obs_value, obs_weight):
    members, fields, rows, cols = sample_collection.shape
    slots = obs_index.shape[-1]
    dirs, tiles = members - 1, members * fields
    group_tiles = -(-members // GROUPS) * fields
    padded_tiles = -(-group_tiles // 8) * 8
    pad = -(-members // 16) * 16
    f32 = jnp.float32
    dims = (members, fields, rows, cols, n_lat, n_lon)
    analysis, spread = pl.pallas_call(
        functools.partial(kernel, dims),
        out_shape=(
            jax.ShapeDtypeStruct((members, fields * rows, cols), f32),
            jax.ShapeDtypeStruct((members, members), f32),
        ),
        in_specs=[pl.BlockSpec(memory_space=pltpu.HBM)] * 5,
        out_specs=(
            pl.BlockSpec(memory_space=pltpu.HBM),
            pl.BlockSpec(memory_space=pltpu.VMEM),
        ),
        scratch_shapes=[
            pltpu.VMEM((1, slots), jnp.int32),
            pltpu.VMEM((1, 1), jnp.int32),
            pltpu.VMEM((1, slots), f32),
            pltpu.VMEM((1, slots), f32),
            pltpu.VMEM((members, fields * rows, cols), f32),
            pltpu.VMEM((2, tiles * rows, cols), f32),
            pltpu.VMEM((SUBSTEPS + 1, GROUPS, padded_tiles, cols), f32),
            pltpu.VMEM((SUBSTEPS + 1, GROUPS, padded_tiles, cols), f32),
            pltpu.VMEM((SUBSTEPS, GROUPS, fields * rows, cols), f32),
            pltpu.VMEM((SUBSTEPS, GROUPS, padded_tiles, cols), f32),
            pltpu.VMEM((SUBSTEPS, GROUPS, padded_tiles, cols), f32),
            pltpu.VMEM((SUBSTEPS, GROUPS, fields * rows, cols), f32),
            pltpu.VMEM((SUBSTEPS, GROUPS, fields * rows, cols), f32),
            pltpu.VMEM((pad, rows * cols), f32),
            pltpu.VMEM((rows * cols, slots), jnp.bfloat16),
            pltpu.VMEM((fields * rows, cols), f32),
            pltpu.VMEM((dirs * fields * rows, cols), f32),
            pltpu.VMEM((2 * dirs, fields * rows * cols), jnp.bfloat16),
            pltpu.VMEM((n_lon, dirs, 128), f32),
            pltpu.VMEM((n_lat, dirs, 128), f32),
            pltpu.VMEM((n_lon, dirs, 128), f32),
            pltpu.VMEM((n_lat, dirs, 128), f32),
            pltpu.SemaphoreType.DMA((5,)),
            pltpu.SemaphoreType.DMA((fields,)),
            pltpu.SemaphoreType.DMA((SUBSTEPS, GROUPS, 4)),
            pltpu.SemaphoreType.DMA((SUBSTEPS, GROUPS, 4)),
        ]
        + [pltpu.SemaphoreType.DMA((n,)) for n in (n_lon, n_lon, n_lat, n_lat) * 2],
        compiler_params=pltpu.CompilerParams(
            collective_id=0, has_side_effects=True, vmem_limit_bytes=VMEM_BYTES
        ),
    )(
        sample_collection.reshape(tiles * rows, cols),
        obs_index.reshape(1, slots),
        obs_count.reshape(1, 1),
        obs_value.reshape(1, slots),
        obs_weight.reshape(1, slots),
    )
    return analysis.reshape(sample_collection.shape), spread


def solution(mesh):
    return jax.shard_map(
        functools.partial(on_device, mesh.shape["lat"], mesh.shape["lon"]),
        mesh=mesh,
        in_specs=(
            P(None, None, "lat", "lon"),
            P("lat", "lon", None),
            P("lat", "lon"),
            P("lat", "lon", None),
            P("lat", "lon", None),
        ),
        out_specs=(P(None, None, "lat", "lon"), P()),
        check_vma=False,
    )
```

```python
import functools
import math

import jax
import jax.numpy as jnp
from jax import lax
from jax.experimental import pallas as pl
from jax.experimental.pallas import tpu as pltpu
from jax.sharding import PartitionSpec as P

SUBSTEPS = 4

time_step = 0.15
coriolis_scale = 0.5
grav_low = 0.5
depth_top = 4.0
depth_low = 6.0
forget = 0.9
highest = lax.Precision.HIGHEST
MESH = pl.DeviceIdType.MESH

COPIES = 3
SYS = 64
BATCH = 4
GROUPS = 2
VMEM_BYTES = 32 * 1024 * 1024


def split2(x):
    high = x.astype(jnp.bfloat16)
    low = (x - high.astype(jnp.float32)).astype(jnp.bfloat16)
    return high, low


def split3(x):
    high = x.astype(jnp.bfloat16)
    rest = x - high.astype(jnp.float32)
    mid = rest.astype(jnp.bfloat16)
    low = (rest - mid.astype(jnp.float32)).astype(jnp.bfloat16)
    return high, mid, low


def dot(a, b):
    return jnp.dot(a, b, preferred_element_type=jnp.float32)


def dot_nt(a, b, precision=None):
    return lax.dot_general(
        a, b, (((1,), (1,)), ((), ())), precision=precision, preferred_element_type=jnp.float32
    )


def kernel(
    dims, x_hbm, index_hbm, count_hbm, value_hbm, weight_hbm,
    out_ref, spread_ref,
    index_ref, count_ref, value_ref, weight_ref,
    state, send_low, send_high, send_cols, from_north, from_south, from_east, from_west,
    surface, selector, means, modes, parts,
    obs_lon, obs_lat, gram_lon, gram_lat, load_sem, halo_send, halo_recv,
    obs_lon_send, obs_lon_recv, obs_lat_send, obs_lat_recv,
    gram_lon_send, gram_lon_recv, gram_lat_send, gram_lat_recv,
):
    members, fields, rows, cols, n_lat, n_lon = dims
    dirs = members - 1
    tiles = members * fields
    cells = rows * cols
    slots = index_ref.shape[1]
    me_lon, me_lat = lax.axis_index("lon"), lax.axis_index("lat")

    def lon_at(d):
        return (lax.rem(me_lon + d + n_lon, n_lon), me_lat)

    def lat_at(d):
        return (me_lon, lax.rem(me_lat + d + n_lat, n_lat))

    partners = [lon_at(d) for d in range(1, n_lon)] + [lat_at(d) for d in range(1, n_lat)]
    barrier = pltpu.get_barrier_semaphore()
    for partner in partners:
        pl.semaphore_signal(barrier, inc=1, device_id=partner, device_id_type=MESH)

    loads = [
        pltpu.make_async_copy(source, target, load_sem.at[number])
        for number, (source, target) in enumerate((
            (x_hbm, state.at[0]),
            (index_hbm, index_ref),
            (count_hbm, count_ref),
            (value_hbm, value_ref),
            (weight_hbm, weight_ref),
        ))
    ]
    for load in loads:
        load.start()

    @pl.when(me_lat == n_lat - 1)
    def _():
        from_north[...] = jnp.zeros_like(from_north)

    @pl.when(me_lat == 0)
    def _():
        from_south[...] = jnp.zeros_like(from_south)

    surface[...] = jnp.zeros_like(surface)
    lane = lax.broadcasted_iota(jnp.int32, (rows, cols), 1)
    row = lax.broadcasted_iota(jnp.int32, (rows, cols), 0)
    half = lane // 2
    first_lane, last_lane = lane == 0, lane == cols - 1
    first_row, last_row = row == 0, row == rows - 1
    even_lane = (lane - 2 * half) == 0
    edge_lane = first_lane | last_lane
    row_number = (row + me_lat * rows).astype(jnp.float32)
    coriolis = coriolis_scale * (2.0 * (row_number + 0.5) / (rows * n_lat) - 1.0)
    turn = time_step * coriolis
    ghost = 0.5 * time_step

    bounds = [members * g // GROUPS for g in range(GROUPS + 1)]

    def put_cols(slot, group, now):
        first, last = bounds[group], bounds[group + 1]
        for field in range(fields):
            packed = jnp.zeros((rows, cols), jnp.float32)
            for member in range(first, last):
                at = (member * fields + field) * rows
                moved = pltpu.roll(state[now, at : at + rows, :], 2 * (member - first) + 1, 1)
                packed = jnp.where(half == member - first, moved, packed)
            send_cols[slot, group, field * rows : (field + 1) * rows, :] = packed
        exchange_start(slot, group, "lon")

    def lines_of(group, field, at_row):
        first, count = bounds[group], bounds[group + 1] - bounds[group]
        at = (first * fields + field) * rows + at_row
        return pl.ds(at, count, stride=fields * rows), pl.ds(field, count, stride=fields)

    def halo_copy(step, group, number):
        source, target, device = (
            (send_low, from_north, lat_at(-1)),
            (send_high, from_south, lat_at(1)),
            (send_cols, from_east, lon_at(-1)),
            (send_cols, from_west, lon_at(1)),
        )[number]
        return pltpu.make_async_remote_copy(
            src_ref=source.at[step, group],
            dst_ref=target.at[step, group],
            send_sem=halo_send.at[step, group, number],
            recv_sem=halo_recv.at[step, group, number],
            device_id=device,
            device_id_type=MESH,
        )

    def exchange_start(step, group, axis):
        if axis == "lon":
            halo_copy(step, group, 2).start()
            halo_copy(step, group, 3).start()
            return

        @pl.when(me_lat > 0)
        def _():
            halo_copy(step, group, 0).start()

        @pl.when(me_lat < n_lat - 1)
        def _():
            halo_copy(step, group, 1).start()

    def exchange_end(step, group, axis):
        if axis == "lon":
            halo_copy(step, group, 2).wait()
            halo_copy(step, group, 3).wait()
            return

        @pl.when(me_lat > 0)
        def _():
            halo_copy(step, group, 0).wait_send()
            halo_copy(step, group, 1).wait_recv()

        @pl.when(me_lat < n_lat - 1)
        def _():
            halo_copy(step, group, 1).wait_send()
            halo_copy(step, group, 0).wait_recv()

    for load in loads:
        load.wait()
    pl.semaphore_wait(barrier, len(partners))
    for group in range(GROUPS):
        for sent, at_row in ((send_low, 0), (send_high, rows - 1)):
            for field in range(fields):
                place, line = lines_of(group, field, at_row)
                sent[0, group, line, :] = state[0, place, :]
        exchange_start(0, group, "lat")
        put_cols(0, group, 0)

    for r in range(rows):
        cell = lax.broadcasted_iota(jnp.int32, (cols, slots), 0) + r * cols
        hit = jnp.where(cell == index_ref[...], 1.0, 0.0)
        selector[r * cols : (r + 1) * cols, :] = hit.astype(jnp.bfloat16)
    live = lax.broadcasted_iota(jnp.int32, (1, slots), 1) < count_ref[...]
    weight = jnp.where(live, weight_ref[...], 0.0) / (slots * n_lat * n_lon)

    def halo_terms(halo, edge, across, side):
        pressure = halo[0] + halo[3]
        terms = []
        for layer, depth in enumerate((depth_top, depth_low)):
            h, u, v = halo[3 * layer : 3 * layer + 3]
            speed = edge[3 * layer + across]
            slope = [(depth + h) * (u, v)[across - 1], speed * u, speed * v]
            slope[across] = slope[across] + pressure
            terms += [0.25 * q - side * d for q, d in zip((h, u, v), slope)]
            pressure = pressure + grav_low * halo[3]
        return terms

    def finish(step, group, later):
        first, last = bounds[group], bounds[group + 1]
        exchange_end(step, group, "lon")
        halo, edge = [], []
        for field in range(fields):
            block = slice(field * rows, (field + 1) * rows)
            from_e = pltpu.roll(from_east[step, group, block, :], cols - 1, 1)
            from_w = pltpu.roll(from_west[step, group, block, :], 1, 1)
            halo.append(jnp.where(even_lane, from_e, from_w))
            edge.append(send_cols[step, group, block, :])
        side = jnp.where(even_lane, ghost, -ghost)
        for field, added in enumerate(halo_terms(halo, edge, 1, side)):
            for member in range(first, last):
                at = (member * fields + field) * rows
                moved = pltpu.roll(added, cols - 1 - 2 * (member - first), 1)
                state[later, at : at + rows, :] += jnp.where(edge_lane, moved, 0.0)

        exchange_end(step, group, "lat")
        for source, sent, at_row, side in (
            (from_north, send_high, rows - 1, ghost),
            (from_south, send_low, 0, -ghost),
        ):
            places, lines = zip(*(lines_of(group, field, at_row) for field in range(fields)))
            halo = [source[step, group, line, :] for line in lines]
            edge = [sent[step, group, line, :] for line in lines]
            for field, added in enumerate(halo_terms(halo, edge, 2, side)):
                moved = state[later, places[field], :] + added
                state[later, places[field], :] = moved
                sent[step + 1, group, lines[field], :] = moved

        @pl.when(step + 1 < SUBSTEPS)
        def _():
            exchange_start(step + 1, group, "lat")
            put_cols(step + 1, group, later)

    def substep(step, carry):
        now, later = lax.rem(step, 2), lax.rem(step + 1, 2)
        for member in range(members):
            here, east, west, north, south = [], [], [], [], []
            for field in range(fields):
                tile = member * fields + field
                q = state[now, tile * rows : (tile + 1) * rows, :]
                here.append(q)
                east.append(jnp.where(last_lane, 0.0, pltpu.roll(q, cols - 1, 1)))
                west.append(jnp.where(first_lane, 0.0, pltpu.roll(q, 1, 1)))
                north.append(jnp.where(last_row, 0.0, pltpu.roll(q, rows - 1, 0)))
                south.append(jnp.where(first_row, 0.0, pltpu.roll(q, 1, 0)))
            dx = [e - w for e, w in zip(east, west)]
            dy = [n - s for n, s in zip(north, south)]
            mean = [0.25 * ((e + w) + (n + s)) for e, w, n, s in zip(east, west, north, south)]
            px_top, py_top = dx[0] + dx[3], dy[0] + dy[3]
            px = (px_top, px_top + grav_low * dx[3])
            py = (py_top, py_top + grav_low * dy[3])
            after = []
            for layer, depth in enumerate((depth_top, depth_low)):
                h, u, v = 3 * layer, 3 * layer + 1, 3 * layer + 2
                flux = ((depth + east[h]) * east[u] - (depth + west[h]) * west[u]) + (
                    (depth + north[h]) * north[v] - (depth + south[h]) * south[v]
                )
                after.append(mean[h] - ghost * flux)
                after.append(
                    mean[u]
                    - ghost * (here[u] * dx[u] + here[v] * dy[u] + px[layer])
                    + turn * here[v]
                )
                after.append(
                    mean[v]
                    - ghost * (here[u] * dx[v] + here[v] * dy[v] + py[layer])
                    - turn * here[u]
                )
            for field in range(fields):
                tile = member * fields + field
                state[later, tile * rows : (tile + 1) * rows, :] = after[field]

        for group in range(GROUPS):
            finish(step, group, later)
        return carry

    lax.fori_loop(0, SUBSTEPS, substep, 0)
    final = SUBSTEPS % 2

    def gather(buffer, me, count, device_of, send, recv):
        copies = []
        for d in range(1, count):
            copy = pltpu.make_async_remote_copy(
                src_ref=buffer.at[me],
                dst_ref=buffer.at[me],
                send_sem=send.at[d],
                recv_sem=recv.at[me],
                device_id=device_of(d),
                device_id_type=MESH,
            )
            copy.start()
            copies.append(copy)

        def total():
            for d in range(1, count):
                other = lax.rem(me + d, count)
                pltpu.make_async_remote_copy(
                    src_ref=buffer.at[other],
                    dst_ref=buffer.at[other],
                    send_sem=send.at[d],
                    recv_sem=recv.at[other],
                    device_id=device_of(d),
                    device_id_type=MESH,
                ).wait_recv()
            for copy in copies:
                copy.wait_send()
            result = buffer[0]
            for i in range(1, count):
                result = result + buffer[i]
            return result

        return total

    pad = surface.shape[0]
    observed = jnp.zeros((3 * pad, slots), jnp.float32)
    for r in range(rows):
        block = slice(r * cols, (r + 1) * cols)
        surface[0:members, block] = (
            state[final, pl.ds(r, members, stride=fields * rows), :]
            + state[final, pl.ds(3 * rows + r, members, stride=fields * rows), :]
        )
        level = jnp.concatenate(split3(surface[:, block]), axis=0)
        observed += dot(level, selector[block, :])
    observed = observed[0:pad] + observed[pad : 2 * pad] + observed[2 * pad : 3 * pad]
    obs_mean = jnp.sum(observed, axis=0, keepdims=True) * (1.0 / members)
    anomaly = observed[0:dirs] - obs_mean
    innovation = value_ref[...] - obs_mean
    top = lax.broadcasted_iota(jnp.int32, (8, slots), 0) == 0
    right = jnp.concatenate(
        [jnp.zeros((SYS, slots), jnp.float32), anomaly, jnp.where(top, innovation, 0.0)], axis=0
    )
    obs_lon[me_lon] = jnp.zeros(obs_lon.shape[1:], jnp.float32)
    obs_lon[me_lon, :, 0 : right.shape[0]] = dot_nt(anomaly * weight, right, highest)
    obs_on_lon = gather(obs_lon, me_lon, n_lon, lon_at, obs_lon_send, obs_lon_recv)

    for field in range(fields):
        total = state[final, field * rows : (field + 1) * rows, :]
        for member in range(1, members):
            at = (member * fields + field) * rows
            total = total + state[final, at : at + rows, :]
        total = total * (1.0 / members)
        means[field * rows : (field + 1) * rows, :] = total
        for member in range(dirs):
            at = (member * fields + field) * rows
            modes[at : at + rows, :] = state[final, at : at + rows, :] - total
    for line in range(fields * rows):
        high, low = split2(modes[pl.ds(line, dirs, stride=fields * rows), :])
        parts[0:dirs, line * cols : (line + 1) * cols] = high
        parts[dirs : 2 * dirs, line * cols : (line + 1) * cols] = low
        parts[2 * dirs : 3 * dirs, line * cols : (line + 1) * cols] = high
    both = parts[0 : 2 * dirs, :]
    gram = dot_nt(both, both)
    gram_lon[me_lon] = jnp.zeros(gram_lon.shape[1:], jnp.float32)
    gram_lon[me_lon, :, 0:dirs] = (
        gram[0:dirs, 0:dirs] + gram[0:dirs, dirs : 2 * dirs] + gram[dirs : 2 * dirs, 0:dirs]
    )
    gram_on_lon = gather(gram_lon, me_lon, n_lon, lon_at, gram_lon_send, gram_lon_recv)

    obs_lat[me_lat] = obs_on_lon()
    obs_on_lat = gather(obs_lat, me_lat, n_lat, lat_at, obs_lat_send, obs_lat_recv)
    gram_lat[me_lat] = gram_on_lon()
    gram_on_lat = gather(gram_lat, me_lat, n_lat, lat_at, gram_lat_send, gram_lat_recv)

    below = lax.broadcasted_iota(jnp.int32, (dirs, 128), 0)
    across = lax.broadcasted_iota(jnp.int32, (dirs, 128), 1)
    identity = sum(jnp.where(across == below + i * dirs, 1.0, 0.0) for i in range(COPIES))
    inside = (across >= SYS) & (across < SYS + dirs)
    gamma = jnp.where(across == below + SYS, 1.0, 0.0) - jnp.where(inside, 1.0 / members, 0.0)
    system = obs_on_lat() + (identity + dirs / forget * gamma)
    for start in range(0, dirs, BATCH):
        batch = [
            jnp.broadcast_to(system[:, SYS + j : SYS + j + 1], system.shape)
            for j in range(start, start + BATCH)
        ]
        for i in range(BATCH):
            j = start + i
            factor = jnp.where(below > j, batch[i] * (1.0 / batch[i][j : j + 1, :]), 0.0)
            for k in range(i + 1, BATCH):
                batch[k] = batch[k] - factor * batch[k][j : j + 1, :]
            system = system - factor * system[j : j + 1, :]
    diagonal = jnp.sum(jnp.where(across == below + SYS, system, 0.0), axis=1, keepdims=True)
    system = system / jnp.sqrt(diagonal)
    solved = system[:, SYS + dirs : SYS + dirs + 1]
    inverse = system[:, 0 : COPIES * dirs]
    weights = jnp.sum(solved * inverse, axis=0, keepdims=True)
    shift = (math.sqrt(members) - 1.0) / dirs
    body = math.sqrt(dirs) * (shift - 1.0) / members
    tail = -math.sqrt(dirs) * math.sqrt(members) / members
    over_rows = jnp.sum(inverse, axis=0, keepdims=True)
    rotation = jnp.concatenate(
        [
            math.sqrt(dirs) * inverse + body * over_rows,
            jnp.broadcast_to(tail * over_rows, (8, COPIES * dirs)),
        ],
        axis=0,
    )
    coefficient = rotation + weights
    rotation = rotation[0:members, 0:dirs]
    mode_gram = gram_on_lat()[:, 0:dirs]
    spread = dot_nt(
        jnp.dot(rotation, mode_gram, precision=highest, preferred_element_type=jnp.float32),
        rotation,
        highest,
    )
    spread_ref[...] = spread * (1.0 / (fields * cells * n_lat * n_lon))

    c_high = coefficient.astype(jnp.bfloat16).astype(jnp.float32)
    part = lax.broadcasted_iota(jnp.int32, coefficient.shape, 1)
    c_parts = jnp.where(part < 2 * dirs, c_high, coefficient - c_high).astype(jnp.bfloat16)
    for field in range(fields):
        update = dot(c_parts, parts[:, field * cells : (field + 1) * cells])
        for r in range(rows):
            line = field * rows + r
            out_ref[:, line, :] = update[0:members, r * cols : (r + 1) * cols] + means[line : line + 1, :]


def on_device(n_lat, n_lon, sample_collection, obs_index, obs_count, obs_value, obs_weight):
    members, fields, rows, cols = sample_collection.shape
    slots = obs_index.shape[-1]
    dirs, tiles = members - 1, members * fields
    group_tiles = -(-members // GROUPS) * fields
    padded_tiles = -(-group_tiles // 8) * 8
    pad = -(-members // 16) * 16
    f32 = jnp.float32
    dims = (members, fields, rows, cols, n_lat, n_lon)
    analysis, spread = pl.pallas_call(
        functools.partial(kernel, dims),
        out_shape=(
            jax.ShapeDtypeStruct((members, fields * rows, cols), f32),
            jax.ShapeDtypeStruct((members, members), f32),
        ),
        in_specs=[pl.BlockSpec(memory_space=pltpu.HBM)] * 5,
        out_specs=(pl.BlockSpec(memory_space=pltpu.VMEM),) * 2,
        scratch_shapes=[
            pltpu.VMEM((1, slots), jnp.int32),
            pltpu.VMEM((1, 1), jnp.int32),
            pltpu.VMEM((1, slots), f32),
            pltpu.VMEM((1, slots), f32),
            pltpu.VMEM((2, tiles * rows, cols), f32),
            pltpu.VMEM((SUBSTEPS + 1, GROUPS, padded_tiles, cols), f32),
            pltpu.VMEM((SUBSTEPS + 1, GROUPS, padded_tiles, cols), f32),
            pltpu.VMEM((SUBSTEPS, GROUPS, fields * rows, cols), f32),
            pltpu.VMEM((SUBSTEPS, GROUPS, padded_tiles, cols), f32),
            pltpu.VMEM((SUBSTEPS, GROUPS, padded_tiles, cols), f32),
            pltpu.VMEM((SUBSTEPS, GROUPS, fields * rows, cols), f32),
            pltpu.VMEM((SUBSTEPS, GROUPS, fields * rows, cols), f32),
            pltpu.VMEM((pad, rows * cols), f32),
            pltpu.VMEM((rows * cols, slots), jnp.bfloat16),
            pltpu.VMEM((fields * rows, cols), f32),
            pltpu.VMEM((dirs * fields * rows, cols), f32),
            pltpu.VMEM((COPIES * dirs, fields * rows * cols), jnp.bfloat16),
            pltpu.VMEM((n_lon, dirs, 128), f32),
            pltpu.VMEM((n_lat, dirs, 128), f32),
            pltpu.VMEM((n_lon, dirs, 128), f32),
            pltpu.VMEM((n_lat, dirs, 128), f32),
            pltpu.SemaphoreType.DMA((5,)),
            pltpu.SemaphoreType.DMA((SUBSTEPS, GROUPS, 4)),
            pltpu.SemaphoreType.DMA((SUBSTEPS, GROUPS, 4)),
        ]
        + [pltpu.SemaphoreType.DMA((n,)) for n in (n_lon, n_lon, n_lat, n_lat) * 2],
        compiler_params=pltpu.CompilerParams(
            collective_id=0, has_side_effects=True, vmem_limit_bytes=VMEM_BYTES
        ),
    )(
        sample_collection.reshape(tiles * rows, cols),
        obs_index.reshape(1, slots),
        obs_count.reshape(1, 1),
        obs_value.reshape(1, slots),
        obs_weight.reshape(1, slots),
    )
    return analysis.reshape(sample_collection.shape), spread


def solution(mesh):
    return jax.shard_map(
        functools.partial(on_device, mesh.shape["lat"], mesh.shape["lon"]),
        mesh=mesh,
        in_specs=(
            P(None, None, "lat", "lon"),
            P("lat", "lon", None),
            P("lat", "lon"),
            P("lat", "lon", None),
            P("lat", "lon", None),
        ),
        out_specs=(P(None, None, "lat", "lon"), P()),
        check_vma=False,
    )
```

```python
import functools
import math

import jax
import jax.numpy as jnp
from jax import lax
from jax.experimental import pallas as pl
from jax.experimental.pallas import tpu as pltpu
from jax.sharding import PartitionSpec as P

SUBSTEPS = 4

time_step = 0.15
coriolis_scale = 0.5
grav_low = 0.5
depth_top = 4.0
depth_low = 6.0
forget = 0.9
highest = lax.Precision.HIGHEST
MESH = pl.DeviceIdType.MESH

COPIES = 3
SYS = 64
BATCH = 4
GROUPS = 2
VMEM_BYTES = 32 * 1024 * 1024


def split2(x):
    high = x.astype(jnp.bfloat16)
    low = (x - high.astype(jnp.float32)).astype(jnp.bfloat16)
    return high, low


def split3(x):
    high = x.astype(jnp.bfloat16)
    rest = x - high.astype(jnp.float32)
    mid = rest.astype(jnp.bfloat16)
    low = (rest - mid.astype(jnp.float32)).astype(jnp.bfloat16)
    return high, mid, low


def dot(a, b):
    return jnp.dot(a, b, preferred_element_type=jnp.float32)


def dot_nt(a, b, precision=None):
    return lax.dot_general(
        a, b, (((1,), (1,)), ((), ())), precision=precision, preferred_element_type=jnp.float32
    )


def kernel(
    dims, x_hbm, index_hbm, count_hbm, value_hbm, weight_hbm,
    out_ref, spread_ref,
    index_ref, count_ref, value_ref, weight_ref,
    state, other, send_low, send_high, send_cols, from_north, from_south, from_east, from_west,
    surface, selector, means, modes, parts,
    obs_lon, obs_lat, gram_lon, gram_lat, load_sem, halo_send, halo_recv,
    obs_lon_send, obs_lon_recv, obs_lat_send, obs_lat_recv,
    gram_lon_send, gram_lon_recv, gram_lat_send, gram_lat_recv,
):
    members, fields, rows, cols, n_lat, n_lon = dims
    dirs = members - 1
    tiles = members * fields
    cells = rows * cols
    slots = index_ref.shape[1]
    me_lon, me_lat = lax.axis_index("lon"), lax.axis_index("lat")

    def lon_at(d):
        return (lax.rem(me_lon + d + n_lon, n_lon), me_lat)

    def lat_at(d):
        return (me_lon, lax.rem(me_lat + d + n_lat, n_lat))

    partners = [lon_at(d) for d in range(1, n_lon)] + [lat_at(d) for d in range(1, n_lat)]
    barrier = pltpu.get_barrier_semaphore()
    for partner in partners:
        pl.semaphore_signal(barrier, inc=1, device_id=partner, device_id_type=MESH)

    loads = [
        pltpu.make_async_copy(source, target, load_sem.at[number])
        for number, (source, target) in enumerate((
            (x_hbm, state),
            (index_hbm, index_ref),
            (count_hbm, count_ref),
            (value_hbm, value_ref),
            (weight_hbm, weight_ref),
        ))
    ]
    for load in loads:
        load.start()

    @pl.when(me_lat == n_lat - 1)
    def _():
        from_north[...] = jnp.zeros_like(from_north)

    @pl.when(me_lat == 0)
    def _():
        from_south[...] = jnp.zeros_like(from_south)

    surface[...] = jnp.zeros_like(surface)
    lane = lax.broadcasted_iota(jnp.int32, (rows, cols), 1)
    row = lax.broadcasted_iota(jnp.int32, (rows, cols), 0)
    half = lane // 2
    first_lane, last_lane = lane == 0, lane == cols - 1
    first_row, last_row = row == 0, row == rows - 1
    even_lane = (lane - 2 * half) == 0
    edge_lane = first_lane | last_lane
    row_number = (row + me_lat * rows).astype(jnp.float32)
    coriolis = coriolis_scale * (2.0 * (row_number + 0.5) / (rows * n_lat) - 1.0)
    turn = time_step * coriolis
    ghost = 0.5 * time_step

    bounds = [members * g // GROUPS for g in range(GROUPS + 1)]

    def put_cols(slot, group, now):
        first, last = bounds[group], bounds[group + 1]
        for field in range(fields):
            packed = jnp.zeros((rows, cols), jnp.float32)
            for member in range(first, last):
                at = (member * fields + field) * rows
                moved = pltpu.roll(now[at : at + rows, :], 2 * (member - first) + 1, 1)
                packed = jnp.where(half == member - first, moved, packed)
            send_cols[slot, group, field * rows : (field + 1) * rows, :] = packed
        exchange_start(slot, group, "lon")

    def lines_of(group, field, at_row):
        first, count = bounds[group], bounds[group + 1] - bounds[group]
        at = (first * fields + field) * rows + at_row
        return pl.ds(at, count, stride=fields * rows), pl.ds(field, count, stride=fields)

    def halo_copy(step, group, number):
        source, target, device = (
            (send_low, from_north, lat_at(-1)),
            (send_high, from_south, lat_at(1)),
            (send_cols, from_east, lon_at(-1)),
            (send_cols, from_west, lon_at(1)),
        )[number]
        return pltpu.make_async_remote_copy(
            src_ref=source.at[step, group],
            dst_ref=target.at[step, group],
            send_sem=halo_send.at[step, group, number],
            recv_sem=halo_recv.at[step, group, number],
            device_id=device,
            device_id_type=MESH,
        )

    def exchange_start(step, group, axis):
        if axis == "lon":
            halo_copy(step, group, 2).start()
            halo_copy(step, group, 3).start()
            return

        @pl.when(me_lat > 0)
        def _():
            halo_copy(step, group, 0).start()

        @pl.when(me_lat < n_lat - 1)
        def _():
            halo_copy(step, group, 1).start()

    def exchange_end(step, group, axis):
        if axis == "lon":
            halo_copy(step, group, 2).wait()
            halo_copy(step, group, 3).wait()
            return

        @pl.when(me_lat > 0)
        def _():
            halo_copy(step, group, 0).wait_send()
            halo_copy(step, group, 1).wait_recv()

        @pl.when(me_lat < n_lat - 1)
        def _():
            halo_copy(step, group, 1).wait_send()
            halo_copy(step, group, 0).wait_recv()

    for load in loads:
        load.wait()
    pl.semaphore_wait(barrier, len(partners))
    for group in range(GROUPS):
        for sent, at_row in ((send_low, 0), (send_high, rows - 1)):
            for field in range(fields):
                place, line = lines_of(group, field, at_row)
                sent[0, group, line, :] = state[place, :]
        exchange_start(0, group, "lat")
        put_cols(0, group, state)

    for r in range(rows):
        cell = lax.broadcasted_iota(jnp.int32, (cols, slots), 0) + r * cols
        hit = jnp.where(cell == index_ref[...], 1.0, 0.0)
        selector[r * cols : (r + 1) * cols, :] = hit.astype(jnp.bfloat16)
    live = lax.broadcasted_iota(jnp.int32, (1, slots), 1) < count_ref[...]
    weight = jnp.where(live, weight_ref[...], 0.0) / (slots * n_lat * n_lon)

    def halo_terms(halo, edge, across, side):
        pressure = halo[0] + halo[3]
        terms = []
        for layer, depth in enumerate((depth_top, depth_low)):
            h, u, v = halo[3 * layer : 3 * layer + 3]
            speed = edge[3 * layer + across]
            slope = [(depth + h) * (u, v)[across - 1], speed * u, speed * v]
            slope[across] = slope[across] + pressure
            terms += [0.25 * q - side * d for q, d in zip((h, u, v), slope)]
            pressure = pressure + grav_low * halo[3]
        return terms

    def finish(step, group, later):
        first, last = bounds[group], bounds[group + 1]
        exchange_end(step, group, "lon")
        halo, edge = [], []
        for field in range(fields):
            block = slice(field * rows, (field + 1) * rows)
            from_e = pltpu.roll(from_east[step, group, block, :], cols - 1, 1)
            from_w = pltpu.roll(from_west[step, group, block, :], 1, 1)
            halo.append(jnp.where(even_lane, from_e, from_w))
            edge.append(send_cols[step, group, block, :])
        side = jnp.where(even_lane, ghost, -ghost)
        for field, added in enumerate(halo_terms(halo, edge, 1, side)):
            tiles_here = [
                slice((member * fields + field) * rows, (member * fields + field + 1) * rows)
                for member in range(first, last)
            ]
            sums = []
            for number, place in enumerate(tiles_here):
                moved = pltpu.roll(added, cols - 1 - 2 * number, 1)
                sums.append(later[place, :] + jnp.where(edge_lane, moved, 0.0))
            for place, value in zip(tiles_here, sums):
                later[place, :] = value

        exchange_end(step, group, "lat")
        for source, sent, at_row, side in (
            (from_north, send_high, rows - 1, ghost),
            (from_south, send_low, 0, -ghost),
        ):
            places, lines = zip(*(lines_of(group, field, at_row) for field in range(fields)))
            halo = [source[step, group, line, :] for line in lines]
            edge = [sent[step, group, line, :] for line in lines]
            sums = [
                later[place, :] + added
                for place, added in zip(places, halo_terms(halo, edge, 2, side))
            ]
            for place, line, value in zip(places, lines, sums):
                later[place, :] = value
                sent[step + 1, group, line, :] = value

        @pl.when(step + 1 < SUBSTEPS)
        def _():
            exchange_start(step + 1, group, "lat")
            put_cols(step + 1, group, later)

    def substep(step, now, later):
        for member in range(members):
            here, east, west, north, south = [], [], [], [], []
            for field in range(fields):
                tile = member * fields + field
                q = now[tile * rows : (tile + 1) * rows, :]
                here.append(q)
                east.append(jnp.where(last_lane, 0.0, pltpu.roll(q, cols - 1, 1)))
                west.append(jnp.where(first_lane, 0.0, pltpu.roll(q, 1, 1)))
                north.append(jnp.where(last_row, 0.0, pltpu.roll(q, rows - 1, 0)))
                south.append(jnp.where(first_row, 0.0, pltpu.roll(q, 1, 0)))
            dx = [e - w for e, w in zip(east, west)]
            dy = [n - s for n, s in zip(north, south)]
            mean = [0.25 * ((e + w) + (n + s)) for e, w, n, s in zip(east, west, north, south)]
            px_top, py_top = dx[0] + dx[3], dy[0] + dy[3]
            px = (px_top, px_top + grav_low * dx[3])
            py = (py_top, py_top + grav_low * dy[3])
            after = []
            for layer, depth in enumerate((depth_top, depth_low)):
                h, u, v = 3 * layer, 3 * layer + 1, 3 * layer + 2
                flux = ((depth + east[h]) * east[u] - (depth + west[h]) * west[u]) + (
                    (depth + north[h]) * north[v] - (depth + south[h]) * south[v]
                )
                after.append(mean[h] - ghost * flux)
                after.append(
                    mean[u]
                    - ghost * (here[u] * dx[u] + here[v] * dy[u] + px[layer])
                    + turn * here[v]
                )
                after.append(
                    mean[v]
                    - ghost * (here[u] * dx[v] + here[v] * dy[v] + py[layer])
                    - turn * here[u]
                )
            for field in range(fields):
                tile = member * fields + field
                later[tile * rows : (tile + 1) * rows, :] = after[field]

        for group in range(GROUPS):
            finish(step, group, later)

    def two_substeps(pair, carry):
        substep(2 * pair, state, other)
        substep(2 * pair + 1, other, state)
        return carry


    lax.fori_loop(0, SUBSTEPS // 2, two_substeps, 0)

    def gather(buffer, me, count, device_of, send, recv):
        copies = []
        for d in range(1, count):
            copy = pltpu.make_async_remote_copy(
                src_ref=buffer.at[me],
                dst_ref=buffer.at[me],
                send_sem=send.at[d],
                recv_sem=recv.at[me],
                device_id=device_of(d),
                device_id_type=MESH,
            )
            copy.start()
            copies.append(copy)

        def total():
            for d in range(1, count):
                other = lax.rem(me + d, count)
                pltpu.make_async_remote_copy(
                    src_ref=buffer.at[other],
                    dst_ref=buffer.at[other],
                    send_sem=send.at[d],
                    recv_sem=recv.at[other],
                    device_id=device_of(d),
                    device_id_type=MESH,
                ).wait_recv()
            for copy in copies:
                copy.wait_send()
            result = buffer[0]
            for i in range(1, count):
                result = result + buffer[i]
            return result

        return total

    pad = surface.shape[0]
    observed = jnp.zeros((3 * pad, slots), jnp.float32)
    for r in range(rows):
        block = slice(r * cols, (r + 1) * cols)
        surface[0:members, block] = (
            state[pl.ds(r, members, stride=fields * rows), :]
            + state[pl.ds(3 * rows + r, members, stride=fields * rows), :]
        )
        level = jnp.concatenate(split3(surface[:, block]), axis=0)
        observed += dot(level, selector[block, :])
    observed = observed[0:pad] + observed[pad : 2 * pad] + observed[2 * pad : 3 * pad]
    obs_mean = jnp.sum(observed, axis=0, keepdims=True) * (1.0 / members)
    anomaly = observed[0:dirs] - obs_mean
    innovation = value_ref[...] - obs_mean
    top = lax.broadcasted_iota(jnp.int32, (8, slots), 0) == 0
    right = jnp.concatenate(
        [jnp.zeros((SYS, slots), jnp.float32), anomaly, jnp.where(top, innovation, 0.0)], axis=0
    )
    obs_lon[me_lon] = jnp.zeros(obs_lon.shape[1:], jnp.float32)
    obs_lon[me_lon, :, 0 : right.shape[0]] = dot_nt(anomaly * weight, right, highest)
    obs_on_lon = gather(obs_lon, me_lon, n_lon, lon_at, obs_lon_send, obs_lon_recv)

    for field in range(fields):
        total = state[field * rows : (field + 1) * rows, :]
        for member in range(1, members):
            at = (member * fields + field) * rows
            total = total + state[at : at + rows, :]
        total = total * (1.0 / members)
        means[field * rows : (field + 1) * rows, :] = total
        for member in range(dirs):
            at = (member * fields + field) * rows
            modes[at : at + rows, :] = state[at : at + rows, :] - total
    for line in range(fields * rows):
        high, low = split2(modes[pl.ds(line, dirs, stride=fields * rows), :])
        parts[0:dirs, line * cols : (line + 1) * cols] = high
        parts[dirs : 2 * dirs, line * cols : (line + 1) * cols] = low
        parts[2 * dirs : 3 * dirs, line * cols : (line + 1) * cols] = high
    both = parts[0 : 2 * dirs, :]
    gram = dot_nt(both, both)
    gram_lon[me_lon] = jnp.zeros(gram_lon.shape[1:], jnp.float32)
    gram_lon[me_lon, :, 0:dirs] = (
        gram[0:dirs, 0:dirs] + gram[0:dirs, dirs : 2 * dirs] + gram[dirs : 2 * dirs, 0:dirs]
    )
    gram_on_lon = gather(gram_lon, me_lon, n_lon, lon_at, gram_lon_send, gram_lon_recv)

    obs_lat[me_lat] = obs_on_lon()
    obs_on_lat = gather(obs_lat, me_lat, n_lat, lat_at, obs_lat_send, obs_lat_recv)
    gram_lat[me_lat] = gram_on_lon()
    gram_on_lat = gather(gram_lat, me_lat, n_lat, lat_at, gram_lat_send, gram_lat_recv)

    below = lax.broadcasted_iota(jnp.int32, (dirs, 128), 0)
    across = lax.broadcasted_iota(jnp.int32, (dirs, 128), 1)
    identity = sum(jnp.where(across == below + i * dirs, 1.0, 0.0) for i in range(COPIES))
    inside = (across >= SYS) & (across < SYS + dirs)
    gamma = jnp.where(across == below + SYS, 1.0, 0.0) - jnp.where(inside, 1.0 / members, 0.0)
    system = obs_on_lat() + (identity + dirs / forget * gamma)
    for start in range(0, dirs, BATCH):
        batch = [
            jnp.broadcast_to(system[:, SYS + j : SYS + j + 1], system.shape)
            for j in range(start, start + BATCH)
        ]
        for i in range(BATCH):
            j = start + i
            factor = jnp.where(below > j, batch[i] * (1.0 / batch[i][j : j + 1, :]), 0.0)
            for k in range(i + 1, BATCH):
                batch[k] = batch[k] - factor * batch[k][j : j + 1, :]
            system = system - factor * system[j : j + 1, :]
    diagonal = jnp.sum(jnp.where(across == below + SYS, system, 0.0), axis=1, keepdims=True)
    system = system / jnp.sqrt(diagonal)
    solved = system[:, SYS + dirs : SYS + dirs + 1]
    inverse = system[:, 0 : COPIES * dirs]
    weights = jnp.sum(solved * inverse, axis=0, keepdims=True)
    shift = (math.sqrt(members) - 1.0) / dirs
    body = math.sqrt(dirs) * (shift - 1.0) / members
    tail = -math.sqrt(dirs) * math.sqrt(members) / members
    over_rows = jnp.sum(inverse, axis=0, keepdims=True)
    rotation = jnp.concatenate(
        [
            math.sqrt(dirs) * inverse + body * over_rows,
            jnp.broadcast_to(tail * over_rows, (8, COPIES * dirs)),
        ],
        axis=0,
    )
    coefficient = rotation + weights
    rotation = rotation[0:members, 0:dirs]
    mode_gram = gram_on_lat()[:, 0:dirs]
    spread = dot_nt(
        jnp.dot(rotation, mode_gram, precision=highest, preferred_element_type=jnp.float32),
        rotation,
        highest,
    )
    spread_ref[...] = spread * (1.0 / (fields * cells * n_lat * n_lon))

    c_high = coefficient.astype(jnp.bfloat16).astype(jnp.float32)
    part = lax.broadcasted_iota(jnp.int32, coefficient.shape, 1)
    c_parts = jnp.where(part < 2 * dirs, c_high, coefficient - c_high).astype(jnp.bfloat16)
    for field in range(fields):
        update = dot(c_parts, parts[:, field * cells : (field + 1) * cells])
        for r in range(rows):
            line = field * rows + r
            out_ref[:, line, :] = update[0:members, r * cols : (r + 1) * cols] + means[line : line + 1, :]


def on_device(n_lat, n_lon, sample_collection, obs_index, obs_count, obs_value, obs_weight):
    members, fields, rows, cols = sample_collection.shape
    slots = obs_index.shape[-1]
    dirs, tiles = members - 1, members * fields
    group_tiles = -(-members // GROUPS) * fields
    padded_tiles = -(-group_tiles // 8) * 8
    pad = -(-members // 16) * 16
    f32 = jnp.float32
    dims = (members, fields, rows, cols, n_lat, n_lon)
    analysis, spread = pl.pallas_call(
        functools.partial(kernel, dims),
        out_shape=(
            jax.ShapeDtypeStruct((members, fields * rows, cols), f32),
            jax.ShapeDtypeStruct((members, members), f32),
        ),
        in_specs=[pl.BlockSpec(memory_space=pltpu.HBM)] * 5,
        out_specs=(pl.BlockSpec(memory_space=pltpu.VMEM),) * 2,
        scratch_shapes=[
            pltpu.VMEM((1, slots), jnp.int32),
            pltpu.VMEM((1, 1), jnp.int32),
            pltpu.VMEM((1, slots), f32),
            pltpu.VMEM((1, slots), f32),
            pltpu.VMEM((tiles * rows, cols), f32),
            pltpu.VMEM((tiles * rows, cols), f32),
            pltpu.VMEM((SUBSTEPS + 1, GROUPS, padded_tiles, cols), f32),
            pltpu.VMEM((SUBSTEPS + 1, GROUPS, padded_tiles, cols), f32),
            pltpu.VMEM((SUBSTEPS, GROUPS, fields * rows, cols), f32),
            pltpu.VMEM((SUBSTEPS, GROUPS, padded_tiles, cols), f32),
            pltpu.VMEM((SUBSTEPS, GROUPS, padded_tiles, cols), f32),
            pltpu.VMEM((SUBSTEPS, GROUPS, fields * rows, cols), f32),
            pltpu.VMEM((SUBSTEPS, GROUPS, fields * rows, cols), f32),
            pltpu.VMEM((pad, rows * cols), f32),
            pltpu.VMEM((rows * cols, slots), jnp.bfloat16),
            pltpu.VMEM((fields * rows, cols), f32),
            pltpu.VMEM((dirs * fields * rows, cols), f32),
            pltpu.VMEM((COPIES * dirs, fields * rows * cols), jnp.bfloat16),
            pltpu.VMEM((n_lon, dirs, 128), f32),
            pltpu.VMEM((n_lat, dirs, 128), f32),
            pltpu.VMEM((n_lon, dirs, 128), f32),
            pltpu.VMEM((n_lat, dirs, 128), f32),
            pltpu.SemaphoreType.DMA((5,)),
            pltpu.SemaphoreType.DMA((SUBSTEPS, GROUPS, 4)),
            pltpu.SemaphoreType.DMA((SUBSTEPS, GROUPS, 4)),
        ]
        + [pltpu.SemaphoreType.DMA((n,)) for n in (n_lon, n_lon, n_lat, n_lat) * 2],
        compiler_params=pltpu.CompilerParams(
            collective_id=0, has_side_effects=True, vmem_limit_bytes=VMEM_BYTES
        ),
    )(
        sample_collection.reshape(tiles * rows, cols),
        obs_index.reshape(1, slots),
        obs_count.reshape(1, 1),
        obs_value.reshape(1, slots),
        obs_weight.reshape(1, slots),
    )
    return analysis.reshape(sample_collection.shape), spread


def solution(mesh):
    return jax.shard_map(
        functools.partial(on_device, mesh.shape["lat"], mesh.shape["lon"]),
        mesh=mesh,
        in_specs=(
            P(None, None, "lat", "lon"),
            P("lat", "lon", None),
            P("lat", "lon"),
            P("lat", "lon", None),
            P("lat", "lon", None),
        ),
        out_specs=(P(None, None, "lat", "lon"), P()),
        check_vma=False,
    )
```

```python
import functools
import math

import jax
import jax.numpy as jnp
from jax import lax
from jax.experimental import pallas as pl
from jax.experimental.pallas import tpu as pltpu
from jax.sharding import PartitionSpec as P

SUBSTEPS = 4

time_step = 0.15
coriolis_scale = 0.5
grav_low = 0.5
depth_top = 4.0
depth_low = 6.0
forget = 0.9
highest = lax.Precision.HIGHEST
MESH = pl.DeviceIdType.MESH

COPIES = 3
SYS = 64
BATCH = 4
GROUPS = 2
VMEM_BYTES = 32 * 1024 * 1024


def split2(x):
    high = x.astype(jnp.bfloat16)
    low = (x - high.astype(jnp.float32)).astype(jnp.bfloat16)
    return high, low


def split3(x):
    high = x.astype(jnp.bfloat16)
    rest = x - high.astype(jnp.float32)
    mid = rest.astype(jnp.bfloat16)
    low = (rest - mid.astype(jnp.float32)).astype(jnp.bfloat16)
    return high, mid, low


def dot(a, b):
    return jnp.dot(a, b, preferred_element_type=jnp.float32)


def dot_nt(a, b, precision=None):
    return lax.dot_general(
        a, b, (((1,), (1,)), ((), ())), precision=precision, preferred_element_type=jnp.float32
    )


def kernel(
    dims, x_hbm, index_hbm, count_hbm, value_hbm, weight_hbm,
    out_ref, spread_ref,
    index_ref, count_ref, value_ref, weight_ref,
    state, other, send_low, send_high, send_cols, from_north, from_south, from_east, from_west,
    surface, selector, means, modes, parts,
    obs_lon, obs_lat, gram_lon, gram_lat, load_sem, halo_send, halo_recv,
    obs_lon_send, obs_lon_recv, obs_lat_send, obs_lat_recv,
    gram_lon_send, gram_lon_recv, gram_lat_send, gram_lat_recv,
):
    members, fields, rows, cols, n_lat, n_lon = dims
    dirs = members - 1
    tiles = members * fields
    cells = rows * cols
    slots = index_ref.shape[1]
    me_lon, me_lat = lax.axis_index("lon"), lax.axis_index("lat")

    def lon_at(d):
        return (lax.rem(me_lon + d + n_lon, n_lon), me_lat)

    def lat_at(d):
        return (me_lon, lax.rem(me_lat + d + n_lat, n_lat))

    partners = [lon_at(d) for d in range(1, n_lon)] + [lat_at(d) for d in range(1, n_lat)]
    barrier = pltpu.get_barrier_semaphore()
    for partner in partners:
        pl.semaphore_signal(barrier, inc=1, device_id=partner, device_id_type=MESH)

    loads = [
        pltpu.make_async_copy(source, target, load_sem.at[number])
        for number, (source, target) in enumerate((
            (x_hbm, state),
            (index_hbm, index_ref),
            (count_hbm, count_ref),
            (value_hbm, value_ref),
            (weight_hbm, weight_ref),
        ))
    ]
    for load in loads:
        load.start()

    @pl.when(me_lat == n_lat - 1)
    def _():
        from_north[...] = jnp.zeros_like(from_north)

    @pl.when(me_lat == 0)
    def _():
        from_south[...] = jnp.zeros_like(from_south)

    surface[...] = jnp.zeros_like(surface)
    lane = lax.broadcasted_iota(jnp.int32, (rows, cols), 1)
    row = lax.broadcasted_iota(jnp.int32, (rows, cols), 0)
    half = lane // 2
    first_lane, last_lane = lane == 0, lane == cols - 1
    first_row, last_row = row == 0, row == rows - 1
    even_lane = (lane - 2 * half) == 0
    edge_lane = first_lane | last_lane
    row_number = (row + me_lat * rows).astype(jnp.float32)
    coriolis = coriolis_scale * (2.0 * (row_number + 0.5) / (rows * n_lat) - 1.0)
    turn = time_step * coriolis
    ghost = 0.5 * time_step

    bounds = [members * g // GROUPS for g in range(GROUPS + 1)]

    def put_cols(slot, group, now):
        first, last = bounds[group], bounds[group + 1]
        for field in range(fields):
            packed = jnp.zeros((rows, cols), jnp.float32)
            for member in range(first, last):
                at = (member * fields + field) * rows
                moved = pltpu.roll(now[at : at + rows, :], 2 * (member - first) + 1, 1)
                packed = jnp.where(half == member - first, moved, packed)
            send_cols[slot, group, field * rows : (field + 1) * rows, :] = packed
        exchange_start(slot, group, "lon")

    def lines_of(group, field, at_row):
        first, count = bounds[group], bounds[group + 1] - bounds[group]
        at = (first * fields + field) * rows + at_row
        return pl.ds(at, count, stride=fields * rows), pl.ds(field, count, stride=fields)

    def halo_copy(step, group, number):
        source, target, device = (
            (send_low, from_north, lat_at(-1)),
            (send_high, from_south, lat_at(1)),
            (send_cols, from_east, lon_at(-1)),
            (send_cols, from_west, lon_at(1)),
        )[number]
        return pltpu.make_async_remote_copy(
            src_ref=source.at[step, group],
            dst_ref=target.at[step, group],
            send_sem=halo_send.at[step, group, number],
            recv_sem=halo_recv.at[step, group, number],
            device_id=device,
            device_id_type=MESH,
        )

    def exchange_start(step, group, axis):
        if axis == "lon":
            halo_copy(step, group, 2).start()
            halo_copy(step, group, 3).start()
            return

        @pl.when(me_lat > 0)
        def _():
            halo_copy(step, group, 0).start()

        @pl.when(me_lat < n_lat - 1)
        def _():
            halo_copy(step, group, 1).start()

    def exchange_end(step, group, axis):
        if axis == "lon":
            halo_copy(step, group, 2).wait_recv()
            halo_copy(step, group, 3).wait_recv()
            return

        @pl.when(me_lat > 0)
        def _():
            halo_copy(step, group, 1).wait_recv()

        @pl.when(me_lat < n_lat - 1)
        def _():
            halo_copy(step, group, 0).wait_recv()

    def exchange_sent(step, group):
        halo_copy(step, group, 2).wait_send()
        halo_copy(step, group, 3).wait_send()

        @pl.when(me_lat > 0)
        def _():
            halo_copy(step, group, 0).wait_send()

        @pl.when(me_lat < n_lat - 1)
        def _():
            halo_copy(step, group, 1).wait_send()

    for load in loads:
        load.wait()
    pl.semaphore_wait(barrier, len(partners))
    for group in range(GROUPS):
        for sent, at_row in ((send_low, 0), (send_high, rows - 1)):
            for field in range(fields):
                place, line = lines_of(group, field, at_row)
                sent[0, group, line, :] = state[place, :]
        exchange_start(0, group, "lat")
        put_cols(0, group, state)

    for r in range(rows):
        cell = lax.broadcasted_iota(jnp.int32, (cols, slots), 0) + r * cols
        hit = jnp.where(cell == index_ref[...], 1.0, 0.0)
        selector[r * cols : (r + 1) * cols, :] = hit.astype(jnp.bfloat16)
    live = lax.broadcasted_iota(jnp.int32, (1, slots), 1) < count_ref[...]
    weight = jnp.where(live, weight_ref[...], 0.0) / (slots * n_lat * n_lon)

    def halo_terms(halo, edge, across, side):
        pressure = halo[0] + halo[3]
        terms = []
        for layer, depth in enumerate((depth_top, depth_low)):
            h, u, v = halo[3 * layer : 3 * layer + 3]
            speed = edge[3 * layer + across]
            slope = [(depth + h) * (u, v)[across - 1], speed * u, speed * v]
            slope[across] = slope[across] + pressure
            terms += [0.25 * q - side * d for q, d in zip((h, u, v), slope)]
            pressure = pressure + grav_low * halo[3]
        return terms

    def finish(step, group, later):
        first, last = bounds[group], bounds[group + 1]
        exchange_end(step, group, "lon")
        halo, edge = [], []
        for field in range(fields):
            block = slice(field * rows, (field + 1) * rows)
            from_e = pltpu.roll(from_east[step, group, block, :], cols - 1, 1)
            from_w = pltpu.roll(from_west[step, group, block, :], 1, 1)
            halo.append(jnp.where(even_lane, from_e, from_w))
            edge.append(send_cols[step, group, block, :])
        side = jnp.where(even_lane, ghost, -ghost)
        for field, added in enumerate(halo_terms(halo, edge, 1, side)):
            tiles_here = [
                slice((member * fields + field) * rows, (member * fields + field + 1) * rows)
                for member in range(first, last)
            ]
            sums = []
            for number, place in enumerate(tiles_here):
                moved = pltpu.roll(added, cols - 1 - 2 * number, 1)
                sums.append(later[place, :] + jnp.where(edge_lane, moved, 0.0))
            for place, value in zip(tiles_here, sums):
                later[place, :] = value

        exchange_end(step, group, "lat")
        for source, sent, at_row, side in (
            (from_north, send_high, rows - 1, ghost),
            (from_south, send_low, 0, -ghost),
        ):
            places, lines = zip(*(lines_of(group, field, at_row) for field in range(fields)))
            halo = [source[step, group, line, :] for line in lines]
            edge = [sent[step, group, line, :] for line in lines]
            sums = [
                later[place, :] + added
                for place, added in zip(places, halo_terms(halo, edge, 2, side))
            ]
            for place, line, value in zip(places, lines, sums):
                later[place, :] = value
                sent[step + 1, group, line, :] = value

        @pl.when(step + 1 < SUBSTEPS)
        def _():
            exchange_start(step + 1, group, "lat")
            put_cols(step + 1, group, later)

    def substep(step, now, later):
        for member in range(members):
            here, east, west, north, south = [], [], [], [], []
            for field in range(fields):
                tile = member * fields + field
                q = now[tile * rows : (tile + 1) * rows, :]
                here.append(q)
                east.append(jnp.where(last_lane, 0.0, pltpu.roll(q, cols - 1, 1)))
                west.append(jnp.where(first_lane, 0.0, pltpu.roll(q, 1, 1)))
                north.append(jnp.where(last_row, 0.0, pltpu.roll(q, rows - 1, 0)))
                south.append(jnp.where(first_row, 0.0, pltpu.roll(q, 1, 0)))
            dx = [e - w for e, w in zip(east, west)]
            dy = [n - s for n, s in zip(north, south)]
            mean = [0.25 * ((e + w) + (n + s)) for e, w, n, s in zip(east, west, north, south)]
            px_top, py_top = dx[0] + dx[3], dy[0] + dy[3]
            px = (px_top, px_top + grav_low * dx[3])
            py = (py_top, py_top + grav_low * dy[3])
            after = []
            for layer, depth in enumerate((depth_top, depth_low)):
                h, u, v = 3 * layer, 3 * layer + 1, 3 * layer + 2
                flux = ((depth + east[h]) * east[u] - (depth + west[h]) * west[u]) + (
                    (depth + north[h]) * north[v] - (depth + south[h]) * south[v]
                )
                after.append(mean[h] - ghost * flux)
                after.append(
                    mean[u]
                    - ghost * (here[u] * dx[u] + here[v] * dy[u] + px[layer])
                    + turn * here[v]
                )
                after.append(
                    mean[v]
                    - ghost * (here[u] * dx[v] + here[v] * dy[v] + py[layer])
                    - turn * here[u]
                )
            for field in range(fields):
                tile = member * fields + field
                later[tile * rows : (tile + 1) * rows, :] = after[field]

        for group in range(GROUPS):
            finish(step, group, later)

    def two_substeps(pair, carry):
        substep(2 * pair, state, other)
        substep(2 * pair + 1, other, state)
        return carry


    lax.fori_loop(0, SUBSTEPS // 2, two_substeps, 0)

    sent_later = []

    def gather(buffer, me, count, device_of, send, recv):
        for d in range(1, count):
            copy = pltpu.make_async_remote_copy(
                src_ref=buffer.at[me],
                dst_ref=buffer.at[me],
                send_sem=send.at[d],
                recv_sem=recv.at[me],
                device_id=device_of(d),
                device_id_type=MESH,
            )
            copy.start()
            sent_later.append(copy)

        def total():
            for d in range(1, count):
                other = lax.rem(me + d, count)
                pltpu.make_async_remote_copy(
                    src_ref=buffer.at[other],
                    dst_ref=buffer.at[other],
                    send_sem=send.at[d],
                    recv_sem=recv.at[other],
                    device_id=device_of(d),
                    device_id_type=MESH,
                ).wait_recv()
            result = buffer[0]
            for i in range(1, count):
                result = result + buffer[i]
            return result

        return total

    pad = surface.shape[0]
    observed = jnp.zeros((3 * pad, slots), jnp.float32)
    for r in range(rows):
        block = slice(r * cols, (r + 1) * cols)
        surface[0:members, block] = (
            state[pl.ds(r, members, stride=fields * rows), :]
            + state[pl.ds(3 * rows + r, members, stride=fields * rows), :]
        )
        level = jnp.concatenate(split3(surface[:, block]), axis=0)
        observed += dot(level, selector[block, :])
    observed = observed[0:pad] + observed[pad : 2 * pad] + observed[2 * pad : 3 * pad]
    obs_mean = jnp.sum(observed, axis=0, keepdims=True) * (1.0 / members)
    anomaly = observed[0:dirs] - obs_mean
    innovation = value_ref[...] - obs_mean
    top = lax.broadcasted_iota(jnp.int32, (8, slots), 0) == 0
    right = jnp.concatenate(
        [jnp.zeros((SYS, slots), jnp.float32), anomaly, jnp.where(top, innovation, 0.0)], axis=0
    )
    obs_lon[me_lon] = jnp.zeros(obs_lon.shape[1:], jnp.float32)
    obs_lon[me_lon, :, 0 : right.shape[0]] = dot_nt(anomaly * weight, right, highest)
    obs_on_lon = gather(obs_lon, me_lon, n_lon, lon_at, obs_lon_send, obs_lon_recv)

    for field in range(fields):
        total = state[field * rows : (field + 1) * rows, :]
        for member in range(1, members):
            at = (member * fields + field) * rows
            total = total + state[at : at + rows, :]
        total = total * (1.0 / members)
        means[field * rows : (field + 1) * rows, :] = total
        for member in range(dirs):
            at = (member * fields + field) * rows
            modes[at : at + rows, :] = state[at : at + rows, :] - total
    for line in range(fields * rows):
        high, low = split2(modes[pl.ds(line, dirs, stride=fields * rows), :])
        parts[0:dirs, line * cols : (line + 1) * cols] = high
        parts[dirs : 2 * dirs, line * cols : (line + 1) * cols] = low
        parts[2 * dirs : 3 * dirs, line * cols : (line + 1) * cols] = high
    both = parts[0 : 2 * dirs, :]
    gram = dot_nt(both, both)
    gram_lon[me_lon] = jnp.zeros(gram_lon.shape[1:], jnp.float32)
    gram_lon[me_lon, :, 0:dirs] = (
        gram[0:dirs, 0:dirs] + gram[0:dirs, dirs : 2 * dirs] + gram[dirs : 2 * dirs, 0:dirs]
    )
    gram_on_lon = gather(gram_lon, me_lon, n_lon, lon_at, gram_lon_send, gram_lon_recv)

    obs_lat[me_lat] = obs_on_lon()
    obs_on_lat = gather(obs_lat, me_lat, n_lat, lat_at, obs_lat_send, obs_lat_recv)
    gram_lat[me_lat] = gram_on_lon()
    gram_on_lat = gather(gram_lat, me_lat, n_lat, lat_at, gram_lat_send, gram_lat_recv)

    below = lax.broadcasted_iota(jnp.int32, (dirs, 128), 0)
    across = lax.broadcasted_iota(jnp.int32, (dirs, 128), 1)
    identity = sum(jnp.where(across == below + i * dirs, 1.0, 0.0) for i in range(COPIES))
    inside = (across >= SYS) & (across < SYS + dirs)
    gamma = jnp.where(across == below + SYS, 1.0, 0.0) - jnp.where(inside, 1.0 / members, 0.0)
    system = obs_on_lat() + (identity + dirs / forget * gamma)
    for start in range(0, dirs, BATCH):
        batch = [
            jnp.broadcast_to(system[:, SYS + j : SYS + j + 1], system.shape)
            for j in range(start, start + BATCH)
        ]
        for i in range(BATCH):
            j = start + i
            factor = jnp.where(below > j, batch[i] * (1.0 / batch[i][j : j + 1, :]), 0.0)
            for k in range(i + 1, BATCH):
                batch[k] = batch[k] - factor * batch[k][j : j + 1, :]
            system = system - factor * system[j : j + 1, :]
    diagonal = jnp.sum(jnp.where(across == below + SYS, system, 0.0), axis=1, keepdims=True)
    system = system / jnp.sqrt(diagonal)
    solved = system[:, SYS + dirs : SYS + dirs + 1]
    inverse = system[:, 0 : COPIES * dirs]
    weights = jnp.sum(solved * inverse, axis=0, keepdims=True)
    shift = (math.sqrt(members) - 1.0) / dirs
    body = math.sqrt(dirs) * (shift - 1.0) / members
    tail = -math.sqrt(dirs) * math.sqrt(members) / members
    over_rows = jnp.sum(inverse, axis=0, keepdims=True)
    rotation = jnp.concatenate(
        [
            math.sqrt(dirs) * inverse + body * over_rows,
            jnp.broadcast_to(tail * over_rows, (8, COPIES * dirs)),
        ],
        axis=0,
    )
    coefficient = rotation + weights
    rotation = rotation[0:members, 0:dirs]
    mode_gram = gram_on_lat()[:, 0:dirs]
    spread = dot_nt(
        jnp.dot(rotation, mode_gram, precision=highest, preferred_element_type=jnp.float32),
        rotation,
        highest,
    )
    spread_ref[...] = spread * (1.0 / (fields * cells * n_lat * n_lon))

    c_high = coefficient.astype(jnp.bfloat16).astype(jnp.float32)
    part = lax.broadcasted_iota(jnp.int32, coefficient.shape, 1)
    c_parts = jnp.where(part < 2 * dirs, c_high, coefficient - c_high).astype(jnp.bfloat16)
    for field in range(fields):
        update = dot(c_parts, parts[:, field * cells : (field + 1) * cells])
        for r in range(rows):
            line = field * rows + r
            out_ref[:, line, :] = update[0:members, r * cols : (r + 1) * cols] + means[line : line + 1, :]

    for copy in sent_later:
        copy.wait_send()
    for step in range(SUBSTEPS):
        for group in range(GROUPS):
            exchange_sent(step, group)


def on_device(n_lat, n_lon, sample_collection, obs_index, obs_count, obs_value, obs_weight):
    members, fields, rows, cols = sample_collection.shape
    slots = obs_index.shape[-1]
    dirs, tiles = members - 1, members * fields
    group_tiles = -(-members // GROUPS) * fields
    padded_tiles = -(-group_tiles // 8) * 8
    pad = -(-members // 16) * 16
    f32 = jnp.float32
    dims = (members, fields, rows, cols, n_lat, n_lon)
    analysis, spread = pl.pallas_call(
        functools.partial(kernel, dims),
        out_shape=(
            jax.ShapeDtypeStruct((members, fields * rows, cols), f32),
            jax.ShapeDtypeStruct((members, members), f32),
        ),
        in_specs=[pl.BlockSpec(memory_space=pltpu.HBM)] * 5,
        out_specs=(pl.BlockSpec(memory_space=pltpu.VMEM),) * 2,
        scratch_shapes=[
            pltpu.VMEM((1, slots), jnp.int32),
            pltpu.VMEM((1, 1), jnp.int32),
            pltpu.VMEM((1, slots), f32),
            pltpu.VMEM((1, slots), f32),
            pltpu.VMEM((tiles * rows, cols), f32),
            pltpu.VMEM((tiles * rows, cols), f32),
            pltpu.VMEM((SUBSTEPS + 1, GROUPS, padded_tiles, cols), f32),
            pltpu.VMEM((SUBSTEPS + 1, GROUPS, padded_tiles, cols), f32),
            pltpu.VMEM((SUBSTEPS, GROUPS, fields * rows, cols), f32),
            pltpu.VMEM((SUBSTEPS, GROUPS, padded_tiles, cols), f32),
            pltpu.VMEM((SUBSTEPS, GROUPS, padded_tiles, cols), f32),
            pltpu.VMEM((SUBSTEPS, GROUPS, fields * rows, cols), f32),
            pltpu.VMEM((SUBSTEPS, GROUPS, fields * rows, cols), f32),
            pltpu.VMEM((pad, rows * cols), f32),
            pltpu.VMEM((rows * cols, slots), jnp.bfloat16),
            pltpu.VMEM((fields * rows, cols), f32),
            pltpu.VMEM((dirs * fields * rows, cols), f32),
            pltpu.VMEM((COPIES * dirs, fields * rows * cols), jnp.bfloat16),
            pltpu.VMEM((n_lon, dirs, 128), f32),
            pltpu.VMEM((n_lat, dirs, 128), f32),
            pltpu.VMEM((n_lon, dirs, 128), f32),
            pltpu.VMEM((n_lat, dirs, 128), f32),
            pltpu.SemaphoreType.DMA((5,)),
            pltpu.SemaphoreType.DMA((SUBSTEPS, GROUPS, 4)),
            pltpu.SemaphoreType.DMA((SUBSTEPS, GROUPS, 4)),
        ]
        + [pltpu.SemaphoreType.DMA((n,)) for n in (n_lon, n_lon, n_lat, n_lat) * 2],
        compiler_params=pltpu.CompilerParams(
            collective_id=0, has_side_effects=True, vmem_limit_bytes=VMEM_BYTES
        ),
    )(
        sample_collection.reshape(tiles * rows, cols),
        obs_index.reshape(1, slots),
        obs_count.reshape(1, 1),
        obs_value.reshape(1, slots),
        obs_weight.reshape(1, slots),
    )
    return analysis.reshape(sample_collection.shape), spread


def solution(mesh):
    return jax.shard_map(
        functools.partial(on_device, mesh.shape["lat"], mesh.shape["lon"]),
        mesh=mesh,
        in_specs=(
            P(None, None, "lat", "lon"),
            P("lat", "lon", None),
            P("lat", "lon"),
            P("lat", "lon", None),
            P("lat", "lon", None),
        ),
        out_specs=(P(None, None, "lat", "lon"), P()),
        check_vma=False,
    )
```
